256 devices in a mesh: tp: 8 (over x, core), dp: 32 (over z, y).
Axes of the slice: x: 4, y: 4, z: 8, core: 2. Of those that a mesh axis runs over, the one named last changes fastest.
Arguments:
- tokens: bfloat16 [1536, 8192], P('tp', 'dp'), may hold values from -60 to 60
- hidden_grad: bfloat16 [1536, 14336], P('dp', 'tp'), may hold values from -60 to 60
- gate_weight: bfloat16 [8192, 14336], P('dp', 'tp'), may hold values from -0.0625 to 0.0625
- up_weight: bfloat16 [8192, 14336], P('dp', 'tp'), may hold values from -0.0625 to 0.0625
- probe: bfloat16 [8192, 14336], P('dp', 'tp'), may hold values from -5 to 5
- moment: float32 [8192, 14336], P('dp', 'tp'), may hold values from -3 to 3
- curvature: float32 [8192, 14336], P('dp', 'tp'), may hold values from 0.02 to 0.2
Outputs:
- new_moment: float32 [8192, 14336], P('dp', 'tp')
- new_curvature: float32 [8192, 14336], P('dp', 'tp')
- update: float32 [8192, 14336], P('dp', 'tp')
The draws below stay inside these ranges and needn't reach their ends.
All inputs are finite; a program needn't handle non-finite values.
Results may differ from the reference program's by a relative error of at most 0.0028.
Values may be sent and summed in bfloat16 or wider, within the bound.
A program may use at most 192 MiB of HBM per device.

```python
import math
import jax
import jax.numpy as jnp
from jax import lax

D = 8192
FF = 14336
TOKENS = 1536


def shaped_field(key, noise_field, tilt):
    rows_total = noise_field.shape[0]
    cols_total = noise_field.shape[1]
    row_key, col_key = jax.random.split(key)
    row_scale = jnp.exp(jax.random.uniform(row_key, (rows_total, 1), jnp.float32, -0.1, 0.1))
    col_scale = jnp.exp(jax.random.uniform(col_key, (1, cols_total), jnp.float32, -1.15, 1.15))
    position = jnp.arange(cols_total, dtype=jnp.float32) / cols_total - 0.5
    rising = jnp.exp(jnp.log(tilt) * position)
    return noise_field * row_scale * col_scale * rising[None, :] / 1.47


def draw_tokens(key, part):
    key = jax.random.fold_in(key, 11)
    noise_key, scale_key = jax.random.split(key)
    noise_field = jax.random.truncated_normal(noise_key, -4.0, 4.0, (TOKENS, D), jnp.float32)
    return shaped_field(scale_key, noise_field, 3.0 ** 0.5).astype(jnp.bfloat16)


def draw_hidden_grad(key, part):
    key = jax.random.fold_in(key, 12)
    noise_key, scale_key = jax.random.split(key)
    noise_field = jax.random.truncated_normal(noise_key, -4.0, 4.0, (TOKENS, FF), jnp.float32)
    return shaped_field(scale_key, noise_field, 3.0 ** 0.5).astype(jnp.bfloat16)


def steps_of(key, shape, cuts, least, largest):
    factor_of, own = 1.0, jax.random.fold_in(key, 6)
    for dim, shards_of in cuts:
        heights = jnp.exp(jax.random.uniform(jax.random.fold_in(own, dim), (shards_of,), jnp.float32, least / len(cuts), largest / len(cuts)))
        factor_of = factor_of * jnp.repeat(heights, shape[dim] // shards_of).reshape([-1 if axis == dim else 1 for axis in range(len(shape))])
    return factor_of


def bell_draw(rng, shape, spread, bound, pieces=(), kind=jnp.bfloat16):
    level = steps_of(rng, shape, pieces, -0.22, 0.18) if pieces else 1.0
    entries = jax.random.normal(rng, shape, jnp.float32) * spread * level
    return jnp.minimum(jnp.maximum(entries, -bound), bound).astype(kind)


def setup_inputs(seed: int = 0) -> dict:
    key_of = jax.random.split(jax.random.key(seed), 8)
    tokens = draw_tokens(jax.random.fold_in(key_of[7], 71), 0)
    hidden_grad = draw_hidden_grad(jax.random.fold_in(key_of[7], 71), 0)
    gate_weight = bell_draw(key_of[2], (D, FF), D ** -0.5, 0.0625, ((0, 32), (1, 8)))
    up_weight = bell_draw(key_of[3], (D, FF), D ** -0.5, 0.0625, ((0, 32), (1, 8)))
    probe = bell_draw(key_of[4], (D, FF), 1.0, 5.0, ((0, 32), (1, 8)))
    moment = bell_draw(key_of[5], (D, FF), 0.5, 3.0, ((0, 32), (1, 8)), jnp.float32)
    curvature = jnp.clip(jnp.exp(math.log(0.2) - 2.3025851 * jax.random.uniform(key_of[6], (D, FF), jnp.float32) ** steps_of(key_of[6], (D, FF), ((0, 32), (1, 8)), -0.2, 0.2)), 0.02, 0.2)
    return dict(tokens=tokens, hidden_grad=hidden_grad, gate_weight=gate_weight, up_weight=up_weight, probe=probe, moment=moment, curvature=curvature)


moment_decay = 0.9
curvature_decay = 0.99
curvature_scale = 2.0
ratio_floor = 0.05
mean_eps = 1e-06

def second_order(gate_pre, up_value, tangent, upstream):
    sigmoid_val = jax.nn.sigmoid(gate_pre)
    first_deriv = sigmoid_val * (1.0 + gate_pre * (1.0 - sigmoid_val))
    second_deriv = sigmoid_val * (1.0 - sigmoid_val) * (2.0 + gate_pre * (1.0 - 2.0 * sigmoid_val))
    scaled = upstream.astype(jnp.float32) * up_value
    grad_rows = (scaled * first_deriv).astype(jnp.bfloat16)
    hess_rows = (scaled * second_deriv * tangent).astype(jnp.bfloat16)
    return (grad_rows, hess_rows)

def reference(tokens, hidden_grad, gate_weight, up_weight, probe, moment, curvature):
    gate_pre = jnp.dot(tokens, gate_weight, preferred_element_type=jnp.float32)
    up_value = jnp.dot(tokens, up_weight, preferred_element_type=jnp.float32)
    tangent = jnp.dot(tokens, probe, preferred_element_type=jnp.float32)
    grad_rows, hess_rows = second_order(gate_pre, up_value, tangent, hidden_grad)
    gradient = jnp.dot(tokens.T, grad_rows, preferred_element_type=jnp.float32)
    curv_product = jnp.dot(tokens.T, hess_rows, preferred_element_type=jnp.float32)
    squares = jnp.sum(gradient * gradient)
    factor = jnp.minimum(1.0, lax.rsqrt(squares / (D * FF) + mean_eps))
    new_moment = moment_decay * moment + (1.0 - moment_decay) * factor * gradient
    new_curvature = curvature_decay * curvature + (1.0 - curvature_decay) * factor * probe.astype(jnp.float32) * curv_product
    update = jnp.clip(new_moment / jnp.maximum(curvature_scale * new_curvature, ratio_floor), -1.0, 1.0)
    return (new_moment, new_curvature, update)
```

```python
import functools

import jax
import jax.numpy as jnp
from jax import lax
from jax.experimental import pallas as pl
from jax.experimental.pallas import tpu as pltpu
from jax.sharding import PartitionSpec as P

D = 8192
FF = 14336

moment_decay = 0.9
curvature_decay = 0.99
curvature_scale = 2.0
ratio_floor = 0.05
mean_eps = 1e-06

NX, NY, NZ = 4, 4, 8
ROWS = 192
HALF = 96
FEAT = 256
DEPTH = NY * FEAT
LANE = 128
TILES = 4

BF = jnp.bfloat16
F32 = jnp.float32


def second_order(gate_pre, up_value, tangent, upstream):
    sigmoid_val = jax.nn.sigmoid(gate_pre)
    first_deriv = sigmoid_val * (1.0 + gate_pre * (1.0 - sigmoid_val))
    second_deriv = sigmoid_val * (1.0 - sigmoid_val) * (2.0 + gate_pre * (1.0 - 2.0 * sigmoid_val))
    scaled = upstream.astype(F32) * up_value
    return (scaled * first_deriv).astype(BF), (scaled * second_deriv * tangent).astype(BF)


def code4(val):
    return ((val * jnp.abs(val)) * (val * val)).astype(BF)


def decode4(coded):
    val = coded.astype(F32)
    root = lax.rsqrt(jnp.maximum(jnp.abs(val), 1e-36))
    return val * root * root * lax.rsqrt(root)


def code2(val):
    return (val * jnp.abs(val)).astype(BF)


def decode2(coded):
    val = coded.astype(F32)
    return val * lax.rsqrt(jnp.maximum(jnp.abs(val), 1e-36))


def kernel(
    tok_in, hid_in, gate_in, up_in, probe_in,
    grad_out, curv_out, squares_out,
    tok, tok_t, wts, hid, rs_out, rs_in, rows, outb, sq, sq_z, sq_y, sq_t,
    tok_l, tok_s, tok_r, w_l, w_s, w_r, hid_l, hid_s, hid_r,
    rs_s, rs_r, ag_s, ag_r, gr_l, gr_s, gr_r, sq_s, sq_r,
):
    tp, dp = lax.axis_index("tp"), lax.axis_index("dp")
    x, c = lax.div(tp, 2), lax.rem(tp, 2)
    z, y = lax.div(dp, NY), lax.rem(dp, NY)

    def mod(val, n):
        return lax.rem(val + n, n)

    def at_y(yy):
        return {"dp": z * NY + yy}

    def at_z(zz):
        return {"dp": zz * NY + y}

    def at_tp(tt):
        return {"tp": tt}

    def first_tile(yy):
        return lax.div(7 * yy + 1 - c, 2)

    def has(yy, t):
        return None if t < TILES - 1 else lax.rem(yy + c, 2) == 0

    def when(cond, fn):
        if cond is None:
            fn()
        else:
            pl.when(cond)(fn)

    def lanes(start, size):
        return pl.ds(pl.multiple_of(start, LANE), size)

    def remote(src, dst, s_sem, r_sem, dev):
        return pltpu.make_async_remote_copy(
            src_ref=src, dst_ref=dst, send_sem=s_sem, recv_sem=r_sem,
            device_id=dev, device_id_type=pl.DeviceIdType.MESH,
        )

    sent = []

    def send(cond, copy):
        when(cond, copy.start)
        sent.append((cond, copy.wait_send))

    def landed(dst, r_sem):
        remote(dst, dst, r_sem, r_sem, at_tp(tp)).wait_recv()

    my_feat = lanes(y * FEAT, FEAT)

    tok_own = pltpu.make_async_copy(tok_in, tok.at[tp, :, my_feat], tok_l)
    tok_own.start()
    weights = (gate_in, up_in, probe_in)
    mine3 = has(y, TILES - 1)

    def mine(t):
        return mine3 if t == TILES - 1 else None

    w_own = {}
    for t in range(TILES):
        for a in range(3):
            w_own[t, a] = pltpu.make_async_copy(
                weights[a].at[:, lanes((first_tile(y) + t) * LANE, LANE)],
                wts.at[t, my_feat, pl.ds(a * LANE, LANE)],
                w_l.at[t, a],
            )
            when(mine(t), w_own[t, a].start)
    my_toks = pl.ds(pl.multiple_of(y * 48, 48), 48)
    hid_own = {}
    for t in range(TILES):
        hid_own[t] = pltpu.make_async_copy(
            hid_in.at[:, lanes((first_tile(y) + t) * LANE, LANE)],
            hid.at[t, my_toks, :],
            hid_l.at[t],
        )
        when(mine(t), hid_own[t].start)

    barrier = pltpu.get_barrier_semaphore()
    peers = [at_y(mod(y + r, NY)) for r in range(1, NY)]
    peers += [at_z(mod(z + r, NZ)) for r in range(1, NZ)]
    peers += [at_tp(mod(tp + r, 8)) for r in range(1, 8)]
    for dev in peers:
        pl.semaphore_signal(barrier, inc=1, device_id=dev, device_id_type=pl.DeviceIdType.MESH)
    pl.semaphore_wait(barrier, len(peers))

    def tok_part(blk, yy):
        return tok.at[blk, :, lanes(yy * FEAT, FEAT)]

    for r in range(1, NY):
        send(None, remote(tok_in, tok_part(tp, y), tok_s.at[r], tok_r.at[r], at_y(mod(y + r, NY))))

    def send_weights(t):
        for r in range(1, NY):
            yy = mod(y + r, NY)
            for a in range(3):
                send(
                    has(yy, t),
                    remote(
                        weights[a].at[:, lanes((first_tile(yy) + t) * LANE, LANE)],
                        wts.at[t, my_feat, pl.ds(a * LANE, LANE)],
                        w_s.at[t, r, a], w_r.at[t, r, a], at_y(yy),
                    ),
                )

    def wait_weights(t):
        def go():
            for a in range(3):
                w_own[t, a].wait()
                for r in range(1, NY):
                    yy = mod(y - r, NY)
                    landed(wts.at[t, lanes(yy * FEAT, FEAT), pl.ds(a * LANE, LANE)], w_r.at[t, r, a])

        when(mine(t), go)

    def send_hidden(t):
        for r in range(1, NY):
            yy = mod(y + r, NY)
            send(
                has(yy, t),
                remote(
                    hid_in.at[:, lanes((first_tile(yy) + t) * LANE, LANE)],
                    hid.at[t, my_toks, :],
                    hid_s.at[t, r], hid_r.at[t, r], at_y(yy),
                ),
            )

    def wait_hidden(t):
        hid_own[t].wait()
        for r in range(1, NY):
            yy = mod(y - r, NY)
            landed(hid.at[t, pl.ds(pl.multiple_of(yy * 48, 48), 48), :], hid_r.at[t, r])

    send_weights(0)

    tok_own.wait()
    for r in range(1, NY):
        landed(tok_part(tp, mod(y - r, NY)), tok_r.at[r])
    other = tp + 1 - 2 * c
    for r in range(1, NX):
        tt = mod(tp + 2 * r, 8)
        send(None, remote(tok.at[tp], tok.at[tp], tok_s.at[3 + r], tok_r.at[3 + r], at_tp(tt)))
    send(None, remote(tok.at[tp], tok.at[tp], tok_s.at[7], tok_r.at[7], at_tp(other)))
    for r in (1, 3, 2):
        blk = mod(tp - 2 * r, 8)
        landed(tok.at[blk], tok_r.at[3 + r])
        send(None, remote(tok.at[blk], tok.at[blk], tok_s.at[7 + r], tok_r.at[7 + r], at_tp(other)))
    wait_weights(0)
    send_weights(1)
    send_hidden(0)
    for r in range(NX):
        landed(tok.at[mod(other - 2 * r, 8)], tok_r.at[7 + r])

    z_next = (mod(z + 1, NZ), mod(z - 1, NZ))
    halves = (pl.ds(0, HALF), pl.ds(HALF, HALF))

    def partial(t, blk):
        return jnp.dot(tok[blk], wts[t], preferred_element_type=F32)

    def rs_send(t, s, d, part):
        send(
            mine(t),
            remote(
                rs_out.at[d, t, s, part, :], rs_in.at[d, t, s, part, :],
                rs_s.at[d, t, s], rs_r.at[d, t, s], at_z(z_next[d]),
            ),
        )

    whole = pl.ds(0, ROWS)

    def rs_step(t, s):
        if s == 0:

            def first():
                val = partial(t, mod(z + 4, NZ))
                for d in range(2):
                    rs_out[d, t, 0, halves[d], :] = code4(val[d * HALF : (d + 1) * HALF])

            when(mine(t), first)
            for d in range(2):
                rs_send(t, 0, d, halves[d])
            return
        for d in range(2):

            def later(d=d):
                blk = mod(z + 4 - s, NZ) if d == 0 else mod(z - 4 + s, NZ)
                val = partial(t, blk)
                part = halves[d] if s == 1 else whole
                landed(rs_in.at[d, t, s - 1, part, :], rs_r.at[d, t, s - 1])
                if s == 1:
                    rs_out[d, t, s, halves[1 - d], :] = code4(val[(1 - d) * HALF : (2 - d) * HALF])
                    rs_out[d, t, s, part, :] = code4(
                        val[d * HALF : (d + 1) * HALF] + decode4(rs_in[d, t, s - 1, part, :])
                    )
                else:
                    rs_out[d, t, s] = code4(val + decode4(rs_in[d, t, s - 1]))

            when(mine(t), later)
            rs_send(t, s, d, whole)

    def ag_send(t, s, d, blk, part):
        send(
            mine(t),
            remote(
                rows.at[t, blk, part, :], rows.at[t, blk, part, :],
                ag_s.at[d, t, s], ag_r.at[d, t, s], at_z(z_next[d]),
            ),
        )

    def rs_last(t):
        def go():
            val = partial(t, z)
            wait_hidden(t)
            for d in range(2):
                landed(rs_in.at[d, t, 3, whole, :], rs_r.at[d, t, 3])
            val = val + decode4(rs_in[0, t, 3]) + decode4(rs_in[1, t, 3])
            grad_rows, hess_rows = second_order(
                val[:, :LANE], val[:, LANE : 2 * LANE], val[:, 2 * LANE :], hid[t]
            )
            rows[t, z, :, pl.ds(0, LANE)] = grad_rows
            rows[t, z, :, pl.ds(LANE, LANE)] = hess_rows

        when(mine(t), go)
        for d in range(2):
            ag_send(t, 0, d, z, whole)

    def ag_step(t, s):
        for d in range(2):
            blk = mod(z - s, NZ) if d == 0 else mod(z + s, NZ)
            when(mine(t), lambda: landed(rows.at[t, blk, whole, :], ag_r.at[d, t, s - 1]))
            ag_send(t, s, d, blk, whole if s < 3 else halves[d])

    def ag_last(t):
        for d in range(2):
            when(mine(t), lambda: landed(rows.at[t, mod(z + 4, NZ), halves[d], :], ag_r.at[d, t, 3]))

    outs = (grad_out, curv_out)
    sq[...] = jnp.zeros_like(sq)

    def products(t):
        for j in (2, 1, 3, 0):
            yy = mod(y + j, NY)

            def go():
                val = jnp.dot(
                    tok_t[pl.ds(pl.multiple_of(yy * FEAT, FEAT), FEAT), :],
                    rows[t].reshape(NZ * ROWS, 2 * LANE),
                    preferred_element_type=F32,
                )
                grad = val[:, :LANE]
                sq[...] += jnp.sum((grad * grad).reshape(FEAT // 8, 8, LANE), axis=0)
                outb[t, j, 0] = grad.astype(BF)
                outb[t, j, 1] = code2(val[:, LANE:])

            when(mine(t), go)
            for a in range(2):
                dst = outs[a].at[:, lanes((first_tile(y) + t) * LANE, LANE)]
                if j:
                    send(mine(t), remote(outb.at[t, j, a], dst, gr_s.at[t, j, a], gr_r.at[t, j, a], at_y(yy)))
                else:
                    own = pltpu.make_async_copy(outb.at[t, j, a], dst, gr_l.at[t, a])
                    when(mine(t), own.start)
                    sent.append((mine(t), own.wait))

    def transpose(i):
        both = tok[pl.ds(2 * i, 2)].reshape(2 * ROWS, DEPTH)
        tok_t[:, pl.ds(i * 2 * ROWS, 2 * ROWS)] = both.T

    rs_step(0, 0)
    transpose(0)
    rs_step(0, 1)
    transpose(1)
    wait_weights(1)
    send_weights(2)
    send_hidden(1)
    rs_step(0, 2)
    rs_step(1, 0)
    transpose(2)
    rs_step(0, 3)
    transpose(3)
    rs_last(0)
    for t in range(1, TILES):
        rs_step(t, 1)
        ag_step(t - 1, 1)
        if t + 1 < TILES:
            wait_weights(t + 1)
            if t + 2 < TILES:
                send_weights(t + 2)
            send_hidden(t + 1)
        rs_step(t, 2)
        ag_step(t - 1, 2)
        rs_step(t, 3)
        ag_step(t - 1, 3)
        if t + 1 < TILES:
            rs_step(t + 1, 0)
        ag_last(t - 1)
        products(t - 1)
        rs_last(t)
    for s in range(1, 4):
        ag_step(TILES - 1, s)
    ag_last(TILES - 1)
    products(TILES - 1)

    def all_sum(buf, n, me, dev_at, base):
        buf[me] = sq[...]
        for r in range(1, n):
            dst = buf.at[me]
            send(None, remote(dst, dst, sq_s.at[base + r], sq_r.at[base + r], dev_at(mod(me + r, n))))
        for r in range(1, n):
            landed(buf.at[mod(me - r, n)], sq_r.at[base + r])
        sq[...] = jnp.sum(buf[...], axis=0)

    all_sum(sq_z, NZ, z, at_z, 0)
    all_sum(sq_y, NY, y, at_y, 8)
    all_sum(sq_t, 8, tp, at_tp, 12)
    squares_out[...] = jnp.broadcast_to(jnp.sum(sq[...]), (8, LANE))

    for t in range(TILES):
        for r in range(1, NY):
            yy = mod(y - r, NY)

            def go():
                for a in range(2):
                    dst = outs[a].at[:, lanes((first_tile(yy) + t) * LANE, LANE)]
                    landed(dst, gr_r.at[t, r, a])

            when(has(yy, t), go)
    for cond, wait in sent:
        when(cond, wait)


def products_of(tokens, hidden_grad, gate_weight, up_weight, probe):
    dma = pltpu.SemaphoreType.DMA
    hbm = pl.BlockSpec(memory_space=pl.ANY)
    return pl.pallas_call(
        kernel,
        out_shape=(
            jax.ShapeDtypeStruct((FEAT, 14 * LANE), BF),
            jax.ShapeDtypeStruct((FEAT, 14 * LANE), BF),
            jax.ShapeDtypeStruct((8, LANE), F32),
        ),
        in_specs=[hbm] * 5,
        out_specs=(hbm, hbm, pl.BlockSpec(memory_space=pltpu.VMEM)),
        scratch_shapes=[
            pltpu.VMEM((8, ROWS, DEPTH), BF),
            pltpu.VMEM((DEPTH, 8 * ROWS), BF),
            pltpu.VMEM((TILES, DEPTH, 3 * LANE), BF),
            pltpu.VMEM((TILES, ROWS, LANE), BF),
            pltpu.VMEM((2, TILES, 4, ROWS, 3 * LANE), BF),
            pltpu.VMEM((2, TILES, 4, ROWS, 3 * LANE), BF),
            pltpu.VMEM((TILES, NZ, ROWS, 2 * LANE), BF),
            pltpu.VMEM((TILES, NY, 2, FEAT, LANE), BF),
            pltpu.VMEM((8, LANE), F32),
            pltpu.VMEM((NZ, 8, LANE), F32),
            pltpu.VMEM((NY, 8, LANE), F32),
            pltpu.VMEM((8, 8, LANE), F32),
            dma, dma((11,)), dma((11,)),
            dma((TILES, 3)), dma((TILES, NY, 3)), dma((TILES, NY, 3)),
            dma((TILES,)), dma((TILES, NY)), dma((TILES, NY)),
            dma((2, TILES, 4)), dma((2, TILES, 4)), dma((2, TILES, 4)), dma((2, TILES, 4)),
            dma((TILES, 2)), dma((TILES, NY, 2)), dma((TILES, NY, 2)),
            dma((20,)), dma((20,)),
        ],
        compiler_params=pltpu.CompilerParams(
            collective_id=0, has_side_effects=True, vmem_limit_bytes=48 * 1024 * 1024
        ),
    )(tokens, hidden_grad, gate_weight, up_weight, probe)


def body(tokens, hidden_grad, gate_weight, up_weight, probe, moment, curvature):
    gradient, curv_coded, squares = products_of(tokens, hidden_grad, gate_weight, up_weight, probe)
    factor = jnp.minimum(1.0, lax.rsqrt(squares[0, 0] / (D * FF) + mean_eps))
    new_moment = moment_decay * moment + (1.0 - moment_decay) * factor * gradient.astype(F32)
    new_curvature = curvature_decay * curvature + (
        1.0 - curvature_decay
    ) * factor * probe.astype(F32) * decode2(curv_coded)
    update = jnp.clip(
        new_moment / jnp.maximum(curvature_scale * new_curvature, ratio_floor), -1.0, 1.0
    )
    return (new_moment, new_curvature, update)


def solution(mesh):
    placed = (
        P("tp", "dp"),
        P("dp", "tp"),
        P("dp", "tp"),
        P("dp", "tp"),
        P("dp", "tp"),
        P("dp", "tp"),
        P("dp", "tp"),
    )
    return jax.shard_map(
        body,
        mesh=mesh,
        in_specs=placed,
        out_specs=(P("dp", "tp"), P("dp", "tp"), P("dp", "tp")),
        check_vma=False,
    )
```

```python
import functools

import jax
import jax.numpy as jnp
from jax import lax
from jax.experimental import pallas as pl
from jax.experimental.pallas import tpu as pltpu
from jax.sharding import PartitionSpec as P

D = 8192
FF = 14336

moment_decay = 0.9
curvature_decay = 0.99
curvature_scale = 2.0
ratio_floor = 0.05
mean_eps = 1e-06

NX, NY, NZ = 4, 4, 8
ROWS = 192
HALF = 96
FEAT = 256
DEPTH = NY * FEAT
LANE = 128
PAIR = 2 * LANE
TILES = 4

BF = jnp.bfloat16
F32 = jnp.float32


def first_part(gate_pre, up_value, upstream):
    sigmoid_val = jax.nn.sigmoid(gate_pre)
    first_deriv = sigmoid_val * (1.0 + gate_pre * (1.0 - sigmoid_val))
    return (upstream.astype(F32) * up_value * first_deriv).astype(BF)


def second_part(gate_pre, up_value, tangent, upstream):
    sigmoid_val = jax.nn.sigmoid(gate_pre)
    second_deriv = sigmoid_val * (1.0 - sigmoid_val) * (2.0 + gate_pre * (1.0 - 2.0 * sigmoid_val))
    return (upstream.astype(F32) * up_value * second_deriv * tangent).astype(BF)


def code4(val):
    return ((val * jnp.abs(val)) * (val * val)).astype(BF)


def decode4(coded):
    val = coded.astype(F32)
    root = lax.rsqrt(jnp.maximum(jnp.abs(val), 1e-36))
    return val * root * root * lax.rsqrt(root)


def code2(val):
    return (val * jnp.abs(val)).astype(BF)


def decode2(coded):
    val = coded.astype(F32)
    return val * lax.rsqrt(jnp.maximum(jnp.abs(val), 1e-36))


STEPS = (
    "U00", "V1", "U10", "U01", "U11", "V2", "U20", "U02", "V3", "U30", "U12", "U21", "U31", "U03", "U13",
    "V4", "V5", "T10", "U22", "U32", "T00", "T11", "U04", "U14", "G00", "T01", "U23", "U33", "T12", "G01",
    "T02", "U24", "U34", "G10", "T13", "G02", "T03", "G11", "T14", "H10", "G03", "T04", "G12", "G04", "H00",
    "P0", "H11", "G13", "H12", "G14", "H01", "P1", "S0", "H13", "H02", "H14", "P3", "H03", "S1", "H04",
    "P2", "S2", "S3",
)


def kernel(
    tok_in, hid_in, gate_in, up_in, probe_in,
    grad_out, curv_out, squares_out,
    tok, wsrc, wu, wt, hid, part_sum, totals, rs_out, rs_in, rows, outb, sq, sq_z, sq_y, sq_t,
    tok_l, ty_s, ty_r, tx_s, tx_r, tc_s, tc_r, src_l, wu_l, wu_s, wu_r, wt_l, wt_s, wt_r,
    hid_l, hid_s, hid_r, rs_s, rs_r, ag_s, ag_r, gr_l, gr_s, gr_r, sq_s, sq_r,
):
    tp, dp = lax.axis_index("tp"), lax.axis_index("dp")
    x, c = lax.div(tp, 2), lax.rem(tp, 2)
    z, y = lax.div(dp, NY), lax.rem(dp, NY)

    def mod(val, n):
        return lax.rem(val + n, n)

    def at_y(yy):
        return {"dp": z * NY + yy}

    def at_z(zz):
        return {"dp": zz * NY + y}

    def at_tp(tt):
        return {"tp": tt}

    def first_tile(yy):
        return lax.div(7 * yy + 1 - c, 2)

    def four(yy):
        return lax.rem(yy + c, 2) == 0

    four_here, three_here = four(y), lax.rem(y + c, 2) == 1

    def one(yy, t):
        return four(yy) if t == TILES - 1 else None

    def widths(yy, p):
        if p == 0:
            return ((None, PAIR),)
        return ((four(yy), PAIR), (lax.rem(yy + c, 2) == 1, LANE))

    def when(cond, fn):
        if cond is None:
            fn()
        else:
            pl.when(cond)(fn)

    def lanes(start, size):
        return pl.ds(pl.multiple_of(start, LANE), size)

    def tile_of(yy, t, size=LANE):
        return lanes((first_tile(yy) + t) * LANE, size)

    def feat(yy):
        return lanes(yy * FEAT, FEAT)

    def remote(src, dst, s_sem, r_sem, dev):
        return pltpu.make_async_remote_copy(
            src_ref=src, dst_ref=dst, send_sem=s_sem, recv_sem=r_sem,
            device_id=dev, device_id_type=pl.DeviceIdType.MESH,
        )

    def send(cond, *args):
        when(cond, remote(*args).start)

    def landed(dst, r_sem):
        remote(dst, dst, r_sem, r_sem, at_tp(tp)).wait_recv()

    def gone(src, s_sem):
        remote(src, src, s_sem, s_sem, at_tp(tp)).wait_send()

    tok_own = pltpu.make_async_copy(tok_in, tok.at[tp, :, feat(y)], tok_l)
    tok_own.start()
    weights = (gate_in, up_in, probe_in)
    staged = [pltpu.make_async_copy(weights[a], wsrc.at[a], src_l.at[a]) for a in range(3)]
    for copy in staged:
        copy.start()
    my_toks = pl.ds(pl.multiple_of(y * 48, 48), 48)

    def hid_own(p, size):
        return pltpu.make_async_copy(
            hid_in.at[:, tile_of(y, 2 * p, size)],
            hid.at[p, my_toks, pl.ds(0, size)],
            hid_l.at[p],
        )

    for p in range(2):
        for cond, size in widths(y, p):
            when(cond, hid_own(p, size).start)

    barrier = pltpu.get_barrier_semaphore()
    peers = [at_y(mod(y + r, NY)) for r in range(1, NY)]
    peers += [at_z(mod(z + r, NZ)) for r in range(1, NZ)]
    peers += [at_tp(mod(tp + r, 8)) for r in range(1, 8)]
    for dev in peers:
        pl.semaphore_signal(barrier, inc=1, device_id=dev, device_id_type=pl.DeviceIdType.MESH)
    pl.semaphore_wait(barrier, len(peers))

    x_next = (mod(tp + 2, 8), mod(tp - 2, 8))
    far = mod(tp + 4, 8)
    other = tp + 1 - 2 * c

    def x_send(blk, r, d, slot):
        ref = tok.at[blk, :, feat(mod(y - r, NY))]
        send(None, ref, ref, tx_s, tx_r.at[slot, r], at_tp(x_next[d]))

    def x_landed(blk, r, slot):
        landed(tok.at[blk, :, feat(mod(y - r, NY))], tx_r.at[slot, r])

    def core_send(blk):
        send(None, tok.at[blk], tok.at[blk], tc_s, tc_r.at[blk], at_tp(other))

    for r in range(1, NY):
        send(None, tok_in, tok.at[tp, :, feat(y)], ty_s, ty_r.at[r], at_y(mod(y + r, NY)))
    tok_own.wait()
    for d in range(2):
        x_send(tp, 0, d, d)
    for copy in staged:
        copy.wait()

    def wu_own(t):
        src, dst = wsrc.at[pl.ds(0, 2), :, tile_of(y, t)], wu.at[t, :, feat(y), :]
        return pltpu.make_async_copy(src, dst, wu_l.at[t])

    def wt_own(p, size):
        src, dst = wsrc.at[2, :, tile_of(y, 2 * p, size)], wt.at[p, feat(y), pl.ds(0, size)]
        return pltpu.make_async_copy(src, dst, wt_l.at[p])

    def send_weights(i):
        for r in (2, 1, 3):
            yy = mod(y + r, NY)
            if i < TILES:
                src, dst = wsrc.at[pl.ds(0, 2), :, tile_of(yy, i)], wu.at[i, :, feat(y), :]
                send(one(yy, i), src, dst, wu_s.at[i], wu_r.at[i, r], at_y(yy))
            else:
                p = i - TILES
                for cond, size in widths(yy, p):
                    src = wsrc.at[2, :, tile_of(yy, 2 * p, size)]
                    dst = wt.at[p, feat(y), pl.ds(0, size)]
                    send(cond, src, dst, wt_s.at[p], wt_r.at[p, r], at_y(yy))
        if i < TILES:
            when(one(y, i), wu_own(i).start)
        else:
            for cond, size in widths(y, i - TILES):
                when(cond, wt_own(i - TILES, size).start)

    def wait_weights(i):
        if i < TILES:

            def go():
                wu_own(i).wait()
                for r in range(1, NY):
                    landed(wu.at[i, :, feat(mod(y - r, NY)), :], wu_r.at[i, r])

            when(one(y, i), go)
            return
        p = i - TILES
        for cond, size in widths(y, p):

            def go():
                wt_own(p, size).wait()
                for r in range(1, NY):
                    landed(wt.at[p, feat(mod(y - r, NY)), pl.ds(0, size)], wt_r.at[p, r])

            when(cond, go)

    def send_hidden(p):
        for r in range(1, NY):
            yy = mod(y + r, NY)
            for cond, size in widths(yy, p):
                src = hid_in.at[:, tile_of(yy, 2 * p, size)]
                dst = hid.at[p, my_toks, pl.ds(0, size)]
                send(cond, src, dst, hid_s.at[p, r], hid_r.at[p, r], at_y(yy))

    def wait_hidden(p):
        for cond, size in widths(y, p):

            def go():
                hid_own(p, size).wait()
                for r in range(1, NY):
                    toks = pl.ds(pl.multiple_of(mod(y - r, NY) * 48, 48), 48)
                    landed(hid.at[p, toks, pl.ds(0, size)], hid_r.at[p, r])

            when(cond, go)

    for r in (1, 3, 2):
        landed(tok.at[tp, :, feat(mod(y - r, NY))], ty_r.at[r])
        for d in range(2):
            x_send(tp, r, d, d)
    send_weights(0)
    core_send(tp)
    for d, r in ((0, 0), (0, 1), (1, 3), (1, 2)):
        x_landed(x_next[1 - d], r, d)
        x_send(x_next[1 - d], r, d, 2)
    for d, rest in ((0, (3, 2)), (1, (0, 1))):
        for r in rest:
            x_landed(x_next[1 - d], r, d)
        core_send(x_next[1 - d])
    send_weights(1)

    def far_tokens():
        for r in (0, 1, 3, 2):
            x_landed(far, r, 2)
        core_send(far)

    far_first = lax.div(mod(z + 4, NZ), 2) == lax.div(far, 2)
    far_later = lax.div(mod(z + 4, NZ), 2) != lax.div(far, 2)

    def wait_block(blk):
        pl.when(lax.rem(blk, 2) != c)(lambda: landed(tok.at[blk], tc_r.at[blk]))

    z_next = (mod(z + 1, NZ), mod(z - 1, NZ))

    def unit_widths(u):
        if u >= TILES:
            return widths(y, u - TILES)
        return ((one(y, u), PAIR),)

    def hop(s):
        return pl.ds(0, 1) if s == 0 else pl.ds(2 * s - 1, 2)

    def dots(u, s):
        if s in (0, 4):
            blks = (mod(z + 4 - s, NZ),)
        else:
            blks = (mod(z + 4 - s, NZ), mod(z - 4 + s, NZ))
        for d, blk in enumerate(blks):
            if u == 0:
                wait_block(blk)
            for cond, size in unit_widths(u):

                def go():
                    if u < TILES:
                        wide = jnp.concatenate([wu[u, a] for a in range(2)], axis=1)
                    else:
                        wide = wt[u - TILES, :, pl.ds(0, size)]
                    val = jnp.dot(tok[blk], wide, preferred_element_type=F32)
                    part_sum[u, d, :, :, pl.ds(0, size)] = val.reshape(2, HALF, size)

                when(cond, go)

    def rs_step(u, s):
        if s == 0:
            dots(u, 0)
        for d in range(2):
            for cond, size in unit_widths(u):
                cols = pl.ds(0, size)

                def go():
                    if s == 0:
                        rs_out[u, d, 0, :, cols] = code4(part_sum[u, 0, d, :, cols])
                        return
                    if s == 1:
                        got, at = rs_in.at[u, d, pl.ds(0, 1), :, cols], pl.ds(d, 1)
                    else:
                        got, at = rs_in.at[u, d, hop(s - 1), :, cols], pl.ds(0, 2)
                    landed(got, rs_r.at[u, d, s - 1])
                    part_sum[u, d, at, :, cols] = part_sum[u, d, at, :, cols] + decode4(got[...])
                    rs_out[u, d, hop(s), :, cols] = code4(part_sum[u, d, :, :, cols])

                when(cond, go)
                src, dst = rs_out.at[u, d, hop(s), :, cols], rs_in.at[u, d, hop(s), :, cols]
                send(cond, src, dst, rs_s.at[u], rs_r.at[u, d, s], at_z(z_next[d]))
        if u == 0 and s == 0:
            pl.when(far_later)(far_tokens)
        dots(u, s + 1)

    def rs_total(u, size):
        cols = pl.ds(0, size)
        val = part_sum[u, 0, :, :, cols]
        for d in range(2):
            got = rs_in.at[u, d, hop(3), :, cols]
            landed(got, rs_r.at[u, d, 3])
            val = val + decode4(got[...])
        return val.reshape(ROWS, size)

    def tile_cols(t):
        return pl.ds((t % 2) * LANE, LANE)

    def last_gate_up(t):
        if t % 2 == 0:
            wait_hidden(t // 2)

        def go():
            val = rs_total(t, PAIR)
            totals[t] = val
            rows[t // 2, z, :, tile_cols(t)] = first_part(
                val[:, :LANE], val[:, LANE:], hid[t // 2, :, tile_cols(t)]
            )

        when(one(y, t), go)

    def last_tangent(p):
        for cond, size in widths(y, p):

            def go():
                val = rs_total(TILES + p, size)
                for i in range(size // LANE):
                    gate_up, cols = totals[2 * p + i], tile_cols(i)
                    rows[2 + p, z, :, cols] = second_part(
                        gate_up[:, :LANE], gate_up[:, LANE:],
                        val[:, i * LANE : (i + 1) * LANE], hid[p, :, cols],
                    )

            when(cond, go)

    def ag_part(s, d):
        return pl.ds(0, ROWS) if s < 3 else pl.ds(d * HALF, HALF)

    def ag_step(u, s):
        for d in range(2):
            back = s if d == 0 else -s
            blk = mod(z - back, NZ)
            for cond, size in widths(y, u % 2):
                cols = pl.ds(0, size)
                if s > 0:
                    got = rows.at[u, blk, ag_part(s - 1, d), cols]
                    when(cond, lambda: landed(got, ag_r.at[u, d, s - 1]))
                if s < 4:
                    ref = rows.at[u, blk, ag_part(s, d), cols]
                    send(cond, ref, ref, ag_s.at[u], ag_r.at[u, d, s], at_z(z_next[d]))

    outs = (grad_out, curv_out)
    sq[...] = jnp.zeros_like(sq)

    def products(u):
        a, p = u // 2, u % 2
        for i, j in enumerate((2, 1, 3, 0)):
            yy = mod(y + j, NY)
            for cond, size in widths(y, p):
                cols = pl.ds(0, size)

                def go():
                    val = lax.dot_general(
                        tok[:, :, feat(yy)].reshape(NZ * ROWS, FEAT),
                        rows[u, :, :, cols].reshape(NZ * ROWS, size),
                        (((0,), (0,)), ((), ())), preferred_element_type=F32,
                    )
                    if a == 0:
                        squared = jnp.sum((val * val).reshape(FEAT // 8, 8, size), axis=0)
                        for k in range(size // LANE):
                            sq[...] += squared[:, k * LANE : (k + 1) * LANE]
                        outb[u, i, :, cols] = val.astype(BF)
                    else:
                        outb[u, i, :, cols] = code2(val)

                when(cond, go)
                src, dst = outb.at[u, i, :, cols], outs[a].at[:, tile_of(y, 2 * p, size)]
                if j:
                    send(cond, src, dst, gr_s.at[u], gr_r.at[u, j], at_y(yy))
                else:
                    when(cond, pltpu.make_async_copy(src, dst, gr_l.at[u]).start)

    stages = ((sq_z, NZ, z, at_z, 0), (sq_y, NY, y, at_y, 8), (sq_t, 8, tp, at_tp, 12))

    def sum_stage(i):
        if i > 0:
            buf, n, me, _, base = stages[i - 1]
            for r in range(1, n):
                landed(buf.at[mod(me - r, n)], sq_r.at[base + r])
            sq[...] = jnp.sum(buf[...], axis=0)
        if i < len(stages):
            buf, n, me, dev_at, base = stages[i]
            buf[me] = sq[...]
            for r in range(1, n):
                dst = buf.at[me]
                send(None, dst, dst, sq_s.at[i], sq_r.at[base + r], dev_at(mod(me + r, n)))

    pl.when(far_first)(far_tokens)
    wait_weights(0)
    send_hidden(0)
    send_weights(2)
    for step in STEPS:
        kind, i = step[0], int(step[1])
        s = int(step[2:] or 0)
        if kind == "V":
            wait_weights(i)
            if i + 2 < TILES + 2:
                send_weights(i + 2)
            if i == 1:
                send_hidden(1)
        elif kind == "U":
            last_gate_up(i) if s == 4 else rs_step(i, s)
        elif kind == "T":
            last_tangent(i) if s == 4 else rs_step(TILES + i, s)
        elif kind == "G":
            ag_step(i, s)
        elif kind == "H":
            ag_step(2 + i, s)
        elif kind == "P":
            products(i)
        else:
            sum_stage(i)
    squares_out[...] = jnp.broadcast_to(jnp.sum(sq[...]), (8, LANE))

    for u in range(4):
        a, p = u // 2, u % 2
        for j in range(1, NY):
            yy = mod(y - j, NY)
            for cond, size in widths(yy, p):
                got = outs[a].at[:, tile_of(yy, 2 * p, size)]
                when(cond, lambda: landed(got, gr_r.at[u, j]))
        for cond, size in widths(y, p):
            cols = pl.ds(0, size)

            def go():
                src, dst = outb.at[u, 3, :, cols], outs[a].at[:, tile_of(y, 2 * p, size)]
                pltpu.make_async_copy(src, dst, gr_l.at[u]).wait()
                gone(outb.at[u, pl.ds(0, 3), :, cols], gr_s.at[u])
                gone(rows.at[u, pl.ds(0, 7), :, cols], ag_s.at[u])

            when(cond, go)
    for u in range(6):
        for cond, size in unit_widths(u):
            when(cond, lambda: gone(rs_out.at[u, :, :, :, pl.ds(0, size)], rs_s.at[u]))
    gone(tok.at[0, :, pl.ds(0, 3 * FEAT)], ty_s)
    gone(tok.at[pl.ds(0, 3)], tx_s)
    gone(tok.at[pl.ds(0, 4)], tc_s)
    for t in range(TILES - 1):
        gone(wu.at[t, :, pl.ds(0, 3 * FEAT), :], wu_s.at[t])
    gone(wt.at[0, pl.ds(0, 3 * FEAT), :], wt_s.at[0])
    for cond, n in ((four_here, 2), (three_here, 4)):
        when(cond, lambda: gone(wu.at[TILES - 1, :, pl.ds(0, n * FEAT // 2), :], wu_s.at[TILES - 1]))
        when(cond, lambda: gone(wt.at[1, pl.ds(0, FEAT * (n + 6) // 4), :], wt_s.at[1]))
    for r in range(1, NY):
        yy = mod(y + r, NY)
        for p in range(2):
            for cond, size in widths(yy, p):
                when(cond, lambda: gone(hid.at[p, my_toks, pl.ds(0, size)], hid_s.at[p, r]))
    for i, (buf, n, _, _, _) in enumerate(stages):
        gone(buf.at[pl.ds(0, n - 1)], sq_s.at[i])


def products_of(tokens, hidden_grad, gate_weight, up_weight, probe):
    dma = pltpu.SemaphoreType.DMA
    hbm = pl.BlockSpec(memory_space=pl.ANY)
    far = pl.BlockSpec(memory_space=pltpu.HBM)
    return pl.pallas_call(
        kernel,
        out_shape=(
            jax.ShapeDtypeStruct((FEAT, 14 * LANE), BF),
            jax.ShapeDtypeStruct((FEAT, 14 * LANE), BF),
            jax.ShapeDtypeStruct((8, LANE), F32),
        ),
        in_specs=[far] * 5,
        out_specs=(hbm, hbm, pl.BlockSpec(memory_space=pltpu.VMEM)),
        scratch_shapes=[
            pltpu.VMEM((8, ROWS, DEPTH), BF),
            pltpu.VMEM((3, FEAT, 14 * LANE), BF),
            pltpu.VMEM((TILES, 2, DEPTH, LANE), BF),
            pltpu.VMEM((2, DEPTH, PAIR), BF),
            pltpu.VMEM((2, ROWS, PAIR), BF),
            pltpu.VMEM((6, 2, 2, HALF, PAIR), F32),
            pltpu.VMEM((TILES, ROWS, PAIR), F32),
            pltpu.VMEM((6, 2, 7, HALF, PAIR), BF),
            pltpu.VMEM((6, 2, 7, HALF, PAIR), BF),
            pltpu.VMEM((4, NZ, ROWS, PAIR), BF),
            pltpu.VMEM((4, NY, FEAT, PAIR), BF),
            pltpu.VMEM((8, LANE), F32),
            pltpu.VMEM((NZ, 8, LANE), F32),
            pltpu.VMEM((NY, 8, LANE), F32),
            pltpu.VMEM((8, 8, LANE), F32),
            dma, dma, dma((NY,)), dma, dma((3, NY)), dma, dma((8,)), dma((3,)),
            dma((TILES,)), dma((TILES,)), dma((TILES, NY)), dma((2,)), dma((2,)), dma((2, NY)),
            dma((2,)), dma((2, NY)), dma((2, NY)),
            dma((6,)), dma((6, 2, 4)), dma((4,)), dma((4, 2, 4)),
            dma((4,)), dma((4,)), dma((4, NY)), dma((3,)), dma((20,)),
        ],
        compiler_params=pltpu.CompilerParams(
            collective_id=0, has_side_effects=True, vmem_limit_bytes=62 * 1024 * 1024
        ),
    )(tokens, hidden_grad, gate_weight, up_weight, probe)


def finish(squares, grad, curv, probe, moment, curvature, moment_out, curvature_out, update_out):
    factor = jnp.minimum(1.0, lax.rsqrt(squares[0:1, 0:1] / (D * FF) + mean_eps))
    new_moment = moment_decay * moment[...] + (1.0 - moment_decay) * factor * grad[...].astype(F32)
    new_curvature = curvature_decay * curvature[...] + (
        1.0 - curvature_decay
    ) * factor * probe[...].astype(F32) * decode2(curv[...])
    moment_out[...] = new_moment
    curvature_out[...] = new_curvature
    update_out[...] = jnp.clip(
        new_moment / jnp.maximum(curvature_scale * new_curvature, ratio_floor), -1.0, 1.0
    )


def body(tokens, hidden_grad, gate_weight, up_weight, probe, moment, curvature):
    gradient, curv_coded, squares = products_of(tokens, hidden_grad, gate_weight, up_weight, probe)
    part = pl.BlockSpec((64, 14 * LANE), lambda i: (i, 0))
    return pl.pallas_call(
        finish,
        grid=(FEAT // 64,),
        out_shape=[jax.ShapeDtypeStruct((FEAT, 14 * LANE), F32)] * 3,
        in_specs=[pl.BlockSpec((8, LANE), lambda i: (0, 0))] + [part] * 5,
        out_specs=[part] * 3,
        compiler_params=pltpu.CompilerParams(vmem_limit_bytes=62 * 1024 * 1024),
    )(squares, gradient, curv_coded, probe, moment, curvature)


def solution(mesh):
    placed = (
        P("tp", "dp"),
        P("dp", "tp"),
        P("dp", "tp"),
        P("dp", "tp"),
        P("dp", "tp"),
        P("dp", "tp"),
        P("dp", "tp"),
    )
    return jax.shard_map(
        body,
        mesh=mesh,
        in_specs=placed,
        out_specs=(P("dp", "tp"), P("dp", "tp"), P("dp", "tp")),
        check_vma=False,
    )
```

```python
import functools

import jax
import jax.numpy as jnp
from jax import lax
from jax.experimental import pallas as pl
from jax.experimental.pallas import tpu as pltpu
from jax.sharding import PartitionSpec as P

D = 8192
FF = 14336

moment_decay = 0.9
curvature_decay = 0.99
curvature_scale = 2.0
ratio_floor = 0.05
mean_eps = 1e-06

NX, NY, NZ = 4, 4, 8
ROWS = 192
HALF = 96
FEAT = 256
DEPTH = NY * FEAT
LANE = 128
PAIR = 2 * LANE
TILES = 4

BF = jnp.bfloat16
F32 = jnp.float32


def first_part(gate_pre, up_value, upstream):
    sigmoid_val = jax.nn.sigmoid(gate_pre)
    first_deriv = sigmoid_val * (1.0 + gate_pre * (1.0 - sigmoid_val))
    return (upstream.astype(F32) * up_value * first_deriv).astype(BF)


def second_part(gate_pre, up_value, tangent, upstream):
    sigmoid_val = jax.nn.sigmoid(gate_pre)
    second_deriv = sigmoid_val * (1.0 - sigmoid_val) * (2.0 + gate_pre * (1.0 - 2.0 * sigmoid_val))
    return (upstream.astype(F32) * up_value * second_deriv * tangent).astype(BF)


def code4(val):
    return ((val * jnp.abs(val)) * (val * val)).astype(BF)


def decode4(coded):
    val = coded.astype(F32)
    root = lax.rsqrt(jnp.maximum(jnp.abs(val), 1e-36))
    return val * root * root * lax.rsqrt(root)


def code2(val):
    return (val * jnp.abs(val)).astype(BF)


def decode2(coded):
    val = coded.astype(F32)
    return val * lax.rsqrt(jnp.maximum(jnp.abs(val), 1e-36))


STEPS = (
    "U00", "V1", "U10", "U01", "U11", "V2", "U20", "U02", "V3", "U30", "U12", "U21", "U31", "U03", "U13",
    "V4", "V5", "T10", "U22", "T00", "U32", "T11", "U04", "U14", "G00", "T01", "U23", "U33", "T12", "G01",
    "T02", "U24", "U34", "G10", "T13", "G02", "T03", "G11", "T14", "H10", "G03", "T04", "G12", "H11", "G04",
    "H00", "P0", "G13", "H12", "G14", "H01", "P1", "S0", "H13", "H02", "H14", "P3", "H03", "S1", "H04",
    "P2", "S2", "S3",
)
ENDS = tuple(int(step[1]) for step in STEPS if step[0] == "P")


def kernel(
    tok_in, hid_in, gate_in, up_in, probe_in,
    grad_out, curv_out, squares_out,
    tok, wsrc, wu, wt, hid, part_sum, totals, rs_out, rs_in, rows, outb, sq, sq_z, sq_y, sq_t,
    tok_l, ty_s, ty_r, tx_s, tx_r, tc_s, tc_r, src_l, wu_l, wu_s, wu_r, wt_l, wt_s, wt_r,
    hid_l, hid_s, hid_r, rs_s, rs_r, ag_s, ag_r, gr_l, gr_s, gr_r, sq_s, sq_r,
):
    tp, dp = lax.axis_index("tp"), lax.axis_index("dp")
    x, c = lax.div(tp, 2), lax.rem(tp, 2)
    z, y = lax.div(dp, NY), lax.rem(dp, NY)

    def mod(val, n):
        return lax.rem(val + n, n)

    def at_y(yy):
        return {"dp": z * NY + yy}

    def at_z(zz):
        return {"dp": zz * NY + y}

    def at_tp(tt):
        return {"tp": tt}

    def first_tile(yy):
        return lax.div(7 * yy + 1 - c, 2)

    def four(yy):
        return lax.rem(yy + c, 2) == 0

    four_here, three_here = four(y), lax.rem(y + c, 2) == 1

    def one(yy, t):
        return four(yy) if t == TILES - 1 else None

    def widths(yy, p):
        if p == 0:
            return ((None, PAIR),)
        return ((four(yy), PAIR), (lax.rem(yy + c, 2) == 1, LANE))

    def when(cond, fn):
        if cond is None:
            fn()
        else:
            pl.when(cond)(fn)

    def lanes(start, size):
        return pl.ds(pl.multiple_of(start, LANE), size)

    def tile_of(yy, t, size=LANE):
        return lanes((first_tile(yy) + t) * LANE, size)

    def feat(yy):
        return lanes(yy * FEAT, FEAT)

    def remote(src, dst, s_sem, r_sem, dev):
        return pltpu.make_async_remote_copy(
            src_ref=src, dst_ref=dst, send_sem=s_sem, recv_sem=r_sem,
            device_id=dev, device_id_type=pl.DeviceIdType.MESH,
        )

    def send(cond, *args):
        when(cond, remote(*args).start)

    def landed(dst, r_sem):
        remote(dst, dst, r_sem, r_sem, at_tp(tp)).wait_recv()

    def gone(src, s_sem):
        remote(src, src, s_sem, s_sem, at_tp(tp)).wait_send()

    tok_own = pltpu.make_async_copy(tok_in, tok.at[tp, :, feat(y)], tok_l)
    tok_own.start()
    weights = (gate_in, up_in, probe_in)
    staged = [pltpu.make_async_copy(weights[a], wsrc.at[a], src_l.at[a]) for a in range(3)]
    for copy in staged:
        copy.start()
    my_toks = pl.ds(pl.multiple_of(y * 48, 48), 48)

    def hid_own(p, size):
        return pltpu.make_async_copy(
            hid_in.at[:, tile_of(y, 2 * p, size)],
            hid.at[p, my_toks, pl.ds(0, size)],
            hid_l.at[p],
        )

    for p in range(2):
        for cond, size in widths(y, p):
            when(cond, hid_own(p, size).start)

    barrier = pltpu.get_barrier_semaphore()
    peers = [at_y(mod(y + r, NY)) for r in range(1, NY)]
    peers += [at_z(mod(z + r, NZ)) for r in range(1, NZ)]
    peers += [at_tp(mod(tp + r, 8)) for r in range(1, 8)]
    for dev in peers:
        pl.semaphore_signal(barrier, inc=1, device_id=dev, device_id_type=pl.DeviceIdType.MESH)
    pl.semaphore_wait(barrier, len(peers))

    x_next = (mod(tp + 2, 8), mod(tp - 2, 8))
    far = mod(tp + 4, 8)
    other = tp + 1 - 2 * c

    def x_send(blk, r, d, slot):
        ref = tok.at[blk, :, feat(mod(y - r, NY))]
        send(None, ref, ref, tx_s, tx_r.at[slot, r], at_tp(x_next[d]))

    def x_landed(blk, r, slot):
        landed(tok.at[blk, :, feat(mod(y - r, NY))], tx_r.at[slot, r])

    def core_send(blk):
        send(None, tok.at[blk], tok.at[blk], tc_s, tc_r.at[blk], at_tp(other))

    for r in (1, 3, 2):
        send(None, tok_in, tok.at[tp, :, feat(y)], ty_s, ty_r.at[r], at_y(mod(y + r, NY)))
    tok_own.wait()
    for d in range(2):
        x_send(tp, 0, d, d)
    for copy in staged:
        copy.wait()

    def wu_own(t):
        src, dst = wsrc.at[pl.ds(0, 2), :, tile_of(y, t)], wu.at[t, :, feat(y), :]
        return pltpu.make_async_copy(src, dst, wu_l.at[t])

    def wt_own(p, size):
        src, dst = wsrc.at[2, :, tile_of(y, 2 * p, size)], wt.at[p, feat(y), pl.ds(0, size)]
        return pltpu.make_async_copy(src, dst, wt_l.at[p])

    def send_weights(i):
        for r in (2, 1, 3):
            yy = mod(y + r, NY)
            if i < TILES:
                src, dst = wsrc.at[pl.ds(0, 2), :, tile_of(yy, i)], wu.at[i, :, feat(y), :]
                send(one(yy, i), src, dst, wu_s.at[i], wu_r.at[i, r], at_y(yy))
            else:
                p = i - TILES
                for cond, size in widths(yy, p):
                    src = wsrc.at[2, :, tile_of(yy, 2 * p, size)]
                    dst = wt.at[p, feat(y), pl.ds(0, size)]
                    send(cond, src, dst, wt_s.at[p], wt_r.at[p, r], at_y(yy))
        if i < TILES:
            when(one(y, i), wu_own(i).start)
        else:
            for cond, size in widths(y, i - TILES):
                when(cond, wt_own(i - TILES, size).start)

    def wait_weights(i):
        if i < TILES:

            def go():
                wu_own(i).wait()
                for r in range(1, NY):
                    landed(wu.at[i, :, feat(mod(y - r, NY)), :], wu_r.at[i, r])

            when(one(y, i), go)
            return
        p = i - TILES
        for cond, size in widths(y, p):

            def go():
                wt_own(p, size).wait()
                for r in range(1, NY):
                    landed(wt.at[p, feat(mod(y - r, NY)), pl.ds(0, size)], wt_r.at[p, r])

            when(cond, go)

    def send_hidden(p):
        for r in range(1, NY):
            yy = mod(y + r, NY)
            for cond, size in widths(yy, p):
                src = hid_in.at[:, tile_of(yy, 2 * p, size)]
                dst = hid.at[p, my_toks, pl.ds(0, size)]
                send(cond, src, dst, hid_s.at[p, r], hid_r.at[p, r], at_y(yy))

    def wait_hidden(p):
        for cond, size in widths(y, p):

            def go():
                hid_own(p, size).wait()
                for r in range(1, NY):
                    toks = pl.ds(pl.multiple_of(mod(y - r, NY) * 48, 48), 48)
                    landed(hid.at[p, toks, pl.ds(0, size)], hid_r.at[p, r])

            when(cond, go)

    for r in (1, 3, 2):
        landed(tok.at[tp, :, feat(mod(y - r, NY))], ty_r.at[r])
        for d in range(2):
            x_send(tp, r, d, d)
    send_weights(0)
    core_send(tp)
    for d, r in ((0, 0), (0, 1), (1, 3), (1, 2)):
        x_landed(x_next[1 - d], r, d)
        x_send(x_next[1 - d], r, d, 2)
    for d, rest in ((0, (3, 2)), (1, (0, 1))):
        for r in rest:
            x_landed(x_next[1 - d], r, d)
        core_send(x_next[1 - d])
    send_weights(1)

    def far_tokens():
        for r in (0, 1, 3, 2):
            x_landed(far, r, 2)
        core_send(far)

    far_first = lax.div(mod(z + 4, NZ), 2) == lax.div(far, 2)
    far_later = lax.div(mod(z + 4, NZ), 2) != lax.div(far, 2)

    def wait_block(blk):
        pl.when(lax.rem(blk, 2) != c)(lambda: landed(tok.at[blk], tc_r.at[blk]))

    z_next = (mod(z + 1, NZ), mod(z - 1, NZ))

    def unit_widths(u):
        if u >= TILES:
            return widths(y, u - TILES)
        return ((one(y, u), PAIR),)

    def hop(s):
        return pl.ds(0, 1) if s == 0 else pl.ds(2 * s - 1, 2)

    def dots(u, s):
        if s in (0, 4):
            blks = (mod(z + 4 - s, NZ),)
        else:
            blks = (mod(z + 4 - s, NZ), mod(z - 4 + s, NZ))
        for d, blk in enumerate(blks):
            if u == 0:
                wait_block(blk)
            for cond, size in unit_widths(u):

                def go():
                    if u < TILES:
                        wide = jnp.concatenate([wu[u, a] for a in range(2)], axis=1)
                    else:
                        wide = wt[u - TILES, :, pl.ds(0, size)]
                    val = jnp.dot(tok[blk], wide, preferred_element_type=F32)
                    part_sum[u, d, :, :, pl.ds(0, size)] = val.reshape(2, HALF, size)

                when(cond, go)

    def rs_step(u, s):
        if s == 0:
            dots(u, 0)
        for d in range(2):
            for cond, size in unit_widths(u):
                cols = pl.ds(0, size)

                def go():
                    if s == 0:
                        rs_out[u, d, 0, :, cols] = code4(part_sum[u, 0, d, :, cols])
                        return
                    if s == 1:
                        got, at = rs_in.at[u, d, pl.ds(0, 1), :, cols], pl.ds(d, 1)
                    else:
                        got, at = rs_in.at[u, d, hop(s - 1), :, cols], pl.ds(0, 2)
                    landed(got, rs_r.at[u, d, s - 1])
                    val = part_sum[u, d, at, :, cols] + decode4(got[...])
                    if s == 1:
                        part_sum[u, d, at, :, cols] = val
                        val = part_sum[u, d, :, :, cols]
                    rs_out[u, d, hop(s), :, cols] = code4(val)

                when(cond, go)
                src, dst = rs_out.at[u, d, hop(s), :, cols], rs_in.at[u, d, hop(s), :, cols]
                send(cond, src, dst, rs_s.at[u], rs_r.at[u, d, s], at_z(z_next[d]))
        if u == 0 and s == 0:
            pl.when(far_later)(far_tokens)
        dots(u, s + 1)

    def rs_total(u, size):
        cols = pl.ds(0, size)
        val = part_sum[u, 0, :, :, cols]
        for d in range(2):
            got = rs_in.at[u, d, hop(3), :, cols]
            landed(got, rs_r.at[u, d, 3])
            val = val + decode4(got[...])
        return val.reshape(ROWS, size)

    def tile_cols(t):
        return pl.ds((t % 2) * LANE, LANE)

    def last_gate_up(t):
        if t % 2 == 0:
            wait_hidden(t // 2)

        def go():
            val = rs_total(t, PAIR)
            totals[t] = val
            rows[t // 2, z, :, tile_cols(t)] = first_part(
                val[:, :LANE], val[:, LANE:], hid[t // 2, :, tile_cols(t)]
            )

        when(one(y, t), go)

    def last_tangent(p):
        for cond, size in widths(y, p):

            def go():
                val = rs_total(TILES + p, size)
                for i in range(size // LANE):
                    gate_up, cols = totals[2 * p + i], tile_cols(i)
                    rows[2 + p, z, :, cols] = second_part(
                        gate_up[:, :LANE], gate_up[:, LANE:],
                        val[:, i * LANE : (i + 1) * LANE], hid[p, :, cols],
                    )

            when(cond, go)

    def ag_part(s, d):
        return pl.ds(0, ROWS) if s < 3 else pl.ds(d * HALF, HALF)

    def ag_step(u, s):
        for d in range(2):
            back = s if d == 0 else -s
            blk = mod(z - back, NZ)
            for cond, size in widths(y, u % 2):
                cols = pl.ds(0, size)
                if s > 0:
                    got = rows.at[u, blk, ag_part(s - 1, d), cols]
                    when(cond, lambda: landed(got, ag_r.at[u, d, s - 1]))
                if s < 4:
                    ref = rows.at[u, blk, ag_part(s, d), cols]
                    send(cond, ref, ref, ag_s.at[u], ag_r.at[u, d, s], at_z(z_next[d]))

    outs = (grad_out, curv_out)
    sq[...] = jnp.zeros_like(sq)

    def products(u):
        a, p = u // 2, u % 2
        for i, j in enumerate((2, 1, 3, 0)):
            yy = mod(y + j, NY)
            for cond, size in widths(y, p):
                cols = pl.ds(0, size)

                def go():
                    val = lax.dot_general(
                        tok[:, :, feat(yy)].reshape(NZ * ROWS, FEAT),
                        rows[u, :, :, cols].reshape(NZ * ROWS, size),
                        (((0,), (0,)), ((), ())), preferred_element_type=F32,
                    )
                    if a == 0:
                        squared = jnp.sum((val * val).reshape(FEAT // 8, 8, size), axis=0)
                        for k in range(size // LANE):
                            sq[...] += squared[:, k * LANE : (k + 1) * LANE]
                        outb[u, i, :, cols] = val.astype(BF)
                    else:
                        outb[u, i, :, cols] = code2(val)

                when(cond, go)
                src, dst = outb.at[u, i, :, cols], outs[a].at[:, tile_of(y, 2 * p, size)]
                if j:
                    send(cond, src, dst, gr_s.at[u], gr_r.at[u, j], at_y(yy))
                else:
                    when(cond, pltpu.make_async_copy(src, dst, gr_l.at[u]).start)

    stages = ((sq_z, NZ, z, at_z, 0), (sq_y, NY, y, at_y, 8), (sq_t, 8, tp, at_tp, 12))

    def sum_stage(i):
        if i > 0:
            buf, n, me, _, base = stages[i - 1]
            for r in range(1, n):
                landed(buf.at[mod(me - r, n)], sq_r.at[base + r])
            sq[...] = jnp.sum(buf[...], axis=0)
        if i < len(stages):
            buf, n, me, dev_at, base = stages[i]
            buf[me] = sq[...]
            for r in range(1, n):
                dst = buf.at[me]
                send(None, dst, dst, sq_s.at[i], sq_r.at[base + r], dev_at(mod(me + r, n)))

    pl.when(far_first)(far_tokens)
    wait_weights(0)
    send_hidden(0)
    send_weights(2)
    for step in STEPS:
        kind, i = step[0], int(step[1])
        s = int(step[2:] or 0)
        if kind == "V":
            wait_weights(i)
            if i + 2 < TILES + 2:
                send_weights(i + 2)
            if i == 1:
                send_hidden(1)
        elif kind == "U":
            last_gate_up(i) if s == 4 else rs_step(i, s)
        elif kind == "T":
            last_tangent(i) if s == 4 else rs_step(TILES + i, s)
        elif kind == "G":
            ag_step(i, s)
        elif kind == "H":
            ag_step(2 + i, s)
        elif kind == "P":
            products(i)
        else:
            sum_stage(i)
    squares_out[...] = jnp.broadcast_to(jnp.sum(sq[...]), (8, LANE))

    gone(tok.at[0, :, pl.ds(0, 3 * FEAT)], ty_s)
    gone(tok.at[pl.ds(0, 3)], tx_s)
    gone(tok.at[pl.ds(0, 4)], tc_s)
    for t in range(TILES - 1):
        gone(wu.at[t, :, pl.ds(0, 3 * FEAT), :], wu_s.at[t])
    gone(wt.at[0, pl.ds(0, 3 * FEAT), :], wt_s.at[0])
    for cond, n in ((four_here, 2), (three_here, 4)):
        when(cond, lambda: gone(wu.at[TILES - 1, :, pl.ds(0, n * FEAT // 2), :], wu_s.at[TILES - 1]))
        when(cond, lambda: gone(wt.at[1, pl.ds(0, FEAT * (n + 6) // 4), :], wt_s.at[1]))
    for r in range(1, NY):
        yy = mod(y + r, NY)
        for p in range(2):
            for cond, size in widths(yy, p):
                when(cond, lambda: gone(hid.at[p, my_toks, pl.ds(0, size)], hid_s.at[p, r]))
    for i, (buf, n, _, _, _) in enumerate(stages):
        gone(buf.at[pl.ds(0, n - 1)], sq_s.at[i])
    for u in range(6):
        for cond, size in unit_widths(u):
            when(cond, lambda: gone(rs_out.at[u, :, :, :, pl.ds(0, size)], rs_s.at[u]))
    for u in range(4):
        for cond, size in widths(y, u % 2):
            when(cond, lambda: gone(rows.at[u, pl.ds(0, 7), :, pl.ds(0, size)], ag_s.at[u]))
    for u in ENDS:
        a, p = u // 2, u % 2
        for cond, size in widths(y, p):
            cols = pl.ds(0, size)

            def go():
                src, dst = outb.at[u, 3, :, cols], outs[a].at[:, tile_of(y, 2 * p, size)]
                pltpu.make_async_copy(src, dst, gr_l.at[u]).wait()
                gone(outb.at[u, pl.ds(0, 3), :, cols], gr_s.at[u])

            when(cond, go)
        for j in range(1, NY):
            yy = mod(y - j, NY)
            for cond, size in widths(yy, p):
                got = outs[a].at[:, tile_of(yy, 2 * p, size)]
                when(cond, lambda: landed(got, gr_r.at[u, j]))


def products_of(tokens, hidden_grad, gate_weight, up_weight, probe):
    dma = pltpu.SemaphoreType.DMA
    hbm = pl.BlockSpec(memory_space=pl.ANY)
    far = pl.BlockSpec(memory_space=pltpu.HBM)
    return pl.pallas_call(
        kernel,
        out_shape=(
            jax.ShapeDtypeStruct((FEAT, 14 * LANE), BF),
            jax.ShapeDtypeStruct((FEAT, 14 * LANE), BF),
            jax.ShapeDtypeStruct((8, LANE), F32),
        ),
        in_specs=[far] * 5,
        out_specs=(hbm, hbm, pl.BlockSpec(memory_space=pltpu.VMEM)),
        scratch_shapes=[
            pltpu.VMEM((8, ROWS, DEPTH), BF),
            pltpu.VMEM((3, FEAT, 14 * LANE), BF),
            pltpu.VMEM((TILES, 2, DEPTH, LANE), BF),
            pltpu.VMEM((2, DEPTH, PAIR), BF),
            pltpu.VMEM((2, ROWS, PAIR), BF),
            pltpu.VMEM((6, 2, 2, HALF, PAIR), F32),
            pltpu.VMEM((TILES, ROWS, PAIR), F32),
            pltpu.VMEM((6, 2, 7, HALF, PAIR), BF),
            pltpu.VMEM((6, 2, 7, HALF, PAIR), BF),
            pltpu.VMEM((4, NZ, ROWS, PAIR), BF),
            pltpu.VMEM((4, NY, FEAT, PAIR), BF),
            pltpu.VMEM((8, LANE), F32),
            pltpu.VMEM((NZ, 8, LANE), F32),
            pltpu.VMEM((NY, 8, LANE), F32),
            pltpu.VMEM((8, 8, LANE), F32),
            dma, dma, dma((NY,)), dma, dma((3, NY)), dma, dma((8,)), dma((3,)),
            dma((TILES,)), dma((TILES,)), dma((TILES, NY)), dma((2,)), dma((2,)), dma((2, NY)),
            dma((2,)), dma((2, NY)), dma((2, NY)),
            dma((6,)), dma((6, 2, 4)), dma((4,)), dma((4, 2, 4)),
            dma((4,)), dma((4,)), dma((4, NY)), dma((3,)), dma((20,)),
        ],
        compiler_params=pltpu.CompilerParams(
            collective_id=0, has_side_effects=True, vmem_limit_bytes=62 * 1024 * 1024
        ),
    )(tokens, hidden_grad, gate_weight, up_weight, probe)


def finish(squares, grad, curv, probe, moment, curvature, moment_out, curvature_out, update_out):
    factor = jnp.minimum(1.0, lax.rsqrt(squares[0:1, 0:1] / (D * FF) + mean_eps))
    new_moment = moment_decay * moment[...] + (1.0 - moment_decay) * factor * grad[...].astype(F32)
    new_curvature = curvature_decay * curvature[...] + (
        1.0 - curvature_decay
    ) * factor * probe[...].astype(F32) * decode2(curv[...])
    moment_out[...] = new_moment
    curvature_out[...] = new_curvature
    update_out[...] = jnp.clip(
        new_moment / jnp.maximum(curvature_scale * new_curvature, ratio_floor), -1.0, 1.0
    )


def body(tokens, hidden_grad, gate_weight, up_weight, probe, moment, curvature):
    gradient, curv_coded, squares = products_of(tokens, hidden_grad, gate_weight, up_weight, probe)
    part = pl.BlockSpec((128, 14 * LANE), lambda i: (i, 0))
    return pl.pallas_call(
        finish,
        grid=(FEAT // 128,),
        out_shape=[jax.ShapeDtypeStruct((FEAT, 14 * LANE), F32)] * 3,
        in_specs=[pl.BlockSpec((8, LANE), lambda i: (0, 0))] + [part] * 5,
        out_specs=[part] * 3,
        compiler_params=pltpu.CompilerParams(vmem_limit_bytes=62 * 1024 * 1024),
    )(squares, gradient, curv_coded, probe, moment, curvature)


def solution(mesh):
    placed = (
        P("tp", "dp"),
        P("dp", "tp"),
        P("dp", "tp"),
        P("dp", "tp"),
        P("dp", "tp"),
        P("dp", "tp"),
        P("dp", "tp"),
    )
    return jax.shard_map(
        body,
        mesh=mesh,
        in_specs=placed,
        out_specs=(P("dp", "tp"), P("dp", "tp"), P("dp", "tp")),
        check_vma=False,
    )
```

```python
import functools

import jax
import jax.numpy as jnp
from jax import lax
from jax.experimental import pallas as pl
from jax.experimental.pallas import tpu as pltpu
from jax.sharding import PartitionSpec as P

D = 8192
FF = 14336

moment_decay = 0.9
curvature_decay = 0.99
curvature_scale = 2.0
ratio_floor = 0.05
mean_eps = 1e-06

NX, NY, NZ = 4, 4, 8
ROWS = 192
HALF = 96
FEAT = 256
DEPTH = NY * FEAT
LANE = 128
PAIR = 2 * LANE
TILES = 4

BF = jnp.bfloat16
F32 = jnp.float32


def first_part(gate_pre, up_value, upstream):
    sigmoid_val = jax.nn.sigmoid(gate_pre)
    first_deriv = sigmoid_val * (1.0 + gate_pre * (1.0 - sigmoid_val))
    return (upstream.astype(F32) * up_value * first_deriv).astype(BF)


def second_part(gate_pre, up_value, tangent, upstream):
    sigmoid_val = jax.nn.sigmoid(gate_pre)
    second_deriv = sigmoid_val * (1.0 - sigmoid_val) * (2.0 + gate_pre * (1.0 - 2.0 * sigmoid_val))
    return (upstream.astype(F32) * up_value * second_deriv * tangent).astype(BF)


def code4(val):
    return ((val * jnp.abs(val)) * (val * val)).astype(BF)


def decode4(coded):
    val = coded.astype(F32)
    root = lax.rsqrt(jnp.maximum(jnp.abs(val), 1e-36))
    return val * root * root * lax.rsqrt(root)


def code2(val):
    return (val * jnp.abs(val)).astype(BF)


def decode2(coded):
    val = coded.astype(F32)
    return val * lax.rsqrt(jnp.maximum(jnp.abs(val), 1e-36))


STEPS = (
    "U00", "V1", "U10", "U01", "U11", "V2", "U20", "U02", "V3", "U30", "U12", "U21", "U31", "U03", "U13",
    "V4", "V5", "T10", "U22", "T00", "U32", "T11", "U04", "U14", "G00", "T01", "U23", "U33", "T12", "G01",
    "T02", "U24", "U34", "G10", "T13", "G02", "T03", "G11", "T14", "H10", "G03", "T04", "G12", "H11", "G04",
    "H00", "P0", "G13", "H12", "G14", "H01", "P1", "S0", "H13", "H02", "H14", "P3", "H03", "S1", "H04",
    "P2", "S2", "S3",
)
ENDS = tuple(int(step[1]) for step in STEPS if step[0] == "P")


def kernel(
    tok_in, hid_in, gate_in, up_in, probe_in,
    grad_out, curv_out, squares_out,
    tok, wsrc, wu, wt, hid, part_sum, totals, rs_out, rs_in, rows, outb, sq, sq_z, sq_y, sq_t,
    tok_l, ty_s, ty_r, tx_s, tx_r, tc_s, tc_r, src_l, wu_l, wu_s, wu_r, wt_l, wt_s, wt_r,
    hid_l, hid_s, hid_r, rs_s, rs_r, ag_s, ag_r, gr_l, gr_s, gr_r, sq_s, sq_r,
):
    tp, dp = lax.axis_index("tp"), lax.axis_index("dp")
    x, c = lax.div(tp, 2), lax.rem(tp, 2)
    z, y = lax.div(dp, NY), lax.rem(dp, NY)

    def mod(val, n):
        return lax.rem(val + n, n)

    def at_y(yy):
        return {"dp": z * NY + yy}

    def at_z(zz):
        return {"dp": zz * NY + y}

    def at_tp(tt):
        return {"tp": tt}

    def first_tile(yy):
        return lax.div(7 * yy + 1 - c, 2)

    def four(yy):
        return lax.rem(yy + c, 2) == 0

    four_here, three_here = four(y), lax.rem(y + c, 2) == 1

    def one(yy, t):
        return four(yy) if t == TILES - 1 else None

    def widths(yy, p):
        if p == 0:
            return ((None, PAIR),)
        return ((four(yy), PAIR), (lax.rem(yy + c, 2) == 1, LANE))

    def when(cond, fn):
        if cond is None:
            fn()
        else:
            pl.when(cond)(fn)

    def lanes(start, size):
        return pl.ds(pl.multiple_of(start, LANE), size)

    def tile_of(yy, t, size=LANE):
        return lanes((first_tile(yy) + t) * LANE, size)

    def feat(yy):
        return lanes(yy * FEAT, FEAT)

    def remote(src, dst, s_sem, r_sem, dev):
        return pltpu.make_async_remote_copy(
            src_ref=src, dst_ref=dst, send_sem=s_sem, recv_sem=r_sem,
            device_id=dev, device_id_type=pl.DeviceIdType.MESH,
        )

    def send(cond, *args):
        when(cond, remote(*args).start)

    def landed(dst, r_sem):
        remote(dst, dst, r_sem, r_sem, at_tp(tp)).wait_recv()

    def gone(src, s_sem):
        remote(src, src, s_sem, s_sem, at_tp(tp)).wait_send()

    tok_own = pltpu.make_async_copy(tok_in, tok.at[tp, :, feat(y)], tok_l)
    tok_own.start()
    weights = (gate_in, up_in, probe_in)
    staged = [pltpu.make_async_copy(weights[a], wsrc.at[a], src_l.at[a]) for a in range(3)]
    for copy in staged:
        copy.start()
    my_toks = pl.ds(pl.multiple_of(y * 48, 48), 48)

    def hid_own(p, size):
        return pltpu.make_async_copy(
            hid_in.at[:, tile_of(y, 2 * p, size)],
            hid.at[p, my_toks, pl.ds(0, size)],
            hid_l.at[p],
        )

    for p in range(2):
        for cond, size in widths(y, p):
            when(cond, hid_own(p, size).start)

    barrier = pltpu.get_barrier_semaphore()
    peers = [at_y(mod(y + r, NY)) for r in range(1, NY)]
    peers += [at_z(mod(z + r, NZ)) for r in range(1, NZ)]
    peers += [at_tp(mod(tp + r, 8)) for r in range(1, 8)]
    for dev in peers:
        pl.semaphore_signal(barrier, inc=1, device_id=dev, device_id_type=pl.DeviceIdType.MESH)
    pl.semaphore_wait(barrier, len(peers))

    x_next = (mod(tp + 2, 8), mod(tp - 2, 8))
    far = mod(tp + 4, 8)
    other = tp + 1 - 2 * c

    def x_send(blk, r, d, slot):
        ref = tok.at[blk, :, feat(mod(y - r, NY))]
        send(None, ref, ref, tx_s, tx_r.at[slot, r], at_tp(x_next[d]))

    def x_landed(blk, r, slot):
        landed(tok.at[blk, :, feat(mod(y - r, NY))], tx_r.at[slot, r])

    def core_send(blk):
        send(None, tok.at[blk], tok.at[blk], tc_s, tc_r.at[blk], at_tp(other))

    for r in (1, 3, 2):
        send(None, tok_in, tok.at[tp, :, feat(y)], ty_s, ty_r.at[r], at_y(mod(y + r, NY)))
    tok_own.wait()
    for d in range(2):
        x_send(tp, 0, d, d)
    for copy in staged:
        copy.wait()

    def wu_own(t):
        src, dst = wsrc.at[pl.ds(0, 2), :, tile_of(y, t)], wu.at[t, :, feat(y), :]
        return pltpu.make_async_copy(src, dst, wu_l.at[t])

    def wt_own(p, size):
        src, dst = wsrc.at[2, :, tile_of(y, 2 * p, size)], wt.at[p, feat(y), pl.ds(0, size)]
        return pltpu.make_async_copy(src, dst, wt_l.at[p])

    def send_weights(i):
        for r in (2, 1, 3):
            yy = mod(y + r, NY)
            if i < TILES:
                src, dst = wsrc.at[pl.ds(0, 2), :, tile_of(yy, i)], wu.at[i, :, feat(y), :]
                send(one(yy, i), src, dst, wu_s.at[i], wu_r.at[i, r], at_y(yy))
            else:
                p = i - TILES
                for cond, size in widths(yy, p):
                    src = wsrc.at[2, :, tile_of(yy, 2 * p, size)]
                    dst = wt.at[p, feat(y), pl.ds(0, size)]
                    send(cond, src, dst, wt_s.at[p], wt_r.at[p, r], at_y(yy))
        if i < TILES:
            when(one(y, i), wu_own(i).start)
        else:
            for cond, size in widths(y, i - TILES):
                when(cond, wt_own(i - TILES, size).start)

    def wait_weights(i):
        if i < TILES:

            def go():
                wu_own(i).wait()
                for r in range(1, NY):
                    landed(wu.at[i, :, feat(mod(y - r, NY)), :], wu_r.at[i, r])

            when(one(y, i), go)
            return
        p = i - TILES
        for cond, size in widths(y, p):

            def go():
                wt_own(p, size).wait()
                for r in range(1, NY):
                    landed(wt.at[p, feat(mod(y - r, NY)), pl.ds(0, size)], wt_r.at[p, r])

            when(cond, go)

    def send_hidden(p):
        for r in range(1, NY):
            yy = mod(y + r, NY)
            for cond, size in widths(yy, p):
                src = hid_in.at[:, tile_of(yy, 2 * p, size)]
                dst = hid.at[p, my_toks, pl.ds(0, size)]
                send(cond, src, dst, hid_s.at[p, r], hid_r.at[p, r], at_y(yy))

    def wait_hidden(p):
        for cond, size in widths(y, p):

            def go():
                hid_own(p, size).wait()
                for r in range(1, NY):
                    toks = pl.ds(pl.multiple_of(mod(y - r, NY) * 48, 48), 48)
                    landed(hid.at[p, toks, pl.ds(0, size)], hid_r.at[p, r])

            when(cond, go)

    for r in (1, 3, 2):
        landed(tok.at[tp, :, feat(mod(y - r, NY))], ty_r.at[r])
        for d in range(2):
            x_send(tp, r, d, d)
        if r == 3:
            send_weights(0)
    core_send(tp)
    for d, r in ((0, 0), (0, 1), (1, 3), (1, 2)):
        x_landed(x_next[1 - d], r, d)
        x_send(x_next[1 - d], r, d, 2)
    for d, rest in ((0, (3, 2)), (1, (0, 1))):
        for r in rest:
            x_landed(x_next[1 - d], r, d)
        core_send(x_next[1 - d])
    send_weights(1)

    def far_tokens():
        for r in (0, 1, 3, 2):
            x_landed(far, r, 2)
        core_send(far)

    far_first = lax.div(mod(z + 4, NZ), 2) == lax.div(far, 2)
    far_later = lax.div(mod(z + 4, NZ), 2) != lax.div(far, 2)

    def wait_block(blk):
        pl.when(lax.rem(blk, 2) != c)(lambda: landed(tok.at[blk], tc_r.at[blk]))

    z_next = (mod(z + 1, NZ), mod(z - 1, NZ))

    def unit_widths(u):
        if u >= TILES:
            return widths(y, u - TILES)
        return ((one(y, u), PAIR),)

    def hop(s):
        return pl.ds(0, 1) if s == 0 else pl.ds(2 * s - 1, 2)

    def dots(u, s):
        if s in (0, 4):
            blks = (mod(z + 4 - s, NZ),)
        else:
            blks = (mod(z + 4 - s, NZ), mod(z - 4 + s, NZ))
        for d, blk in enumerate(blks):
            if u == 0:
                wait_block(blk)
            for cond, size in unit_widths(u):

                def go():
                    if u < TILES:
                        wide = jnp.concatenate([wu[u, a] for a in range(2)], axis=1)
                    else:
                        wide = wt[u - TILES, :, pl.ds(0, size)]
                    val = jnp.dot(tok[blk], wide, preferred_element_type=F32)
                    part_sum[u, d, :, :, pl.ds(0, size)] = val.reshape(2, HALF, size)

                when(cond, go)

    def rs_send(u, d, at, sem):
        for cond, size in unit_widths(u):
            cols = pl.ds(0, size)
            src, dst = rs_out.at[u, d, at, :, cols], rs_in.at[u, d, at, :, cols]
            send(cond, src, dst, rs_s.at[u], rs_r.at[u, d, sem], at_z(z_next[d]))

    def rs_step(u, s):
        if s == 0:
            dots(u, 0)
        for d in range(2):
            at = pl.ds(1 + d, 1) if s == 1 else hop(s)
            for cond, size in unit_widths(u):
                cols = pl.ds(0, size)

                def go():
                    if s == 0:
                        rs_out[u, d, 0, :, cols] = code4(part_sum[u, 0, d, :, cols])
                        return
                    part = pl.ds(d, 1) if s == 1 else pl.ds(0, 2)
                    if s == 2:
                        landed(rs_in.at[u, d, pl.ds(1 + d, 1), :, cols], rs_r.at[u, d, 1])
                        landed(rs_in.at[u, d, pl.ds(2 - d, 1), :, cols], rs_r.at[u, d, 4])
                    else:
                        landed(rs_in.at[u, d, hop(s - 1), :, cols], rs_r.at[u, d, s - 1])
                    val = part_sum[u, d, part, :, cols] + decode4(rs_in[u, d, hop(s - 1), :, cols])
                    rs_out[u, d, at, :, cols] = code4(val)

                when(cond, go)
            rs_send(u, d, at, s)
        if u == 0 and s == 0:
            pl.when(far_later)(far_tokens)
        dots(u, s + 1)
        if s > 0:
            return
        for d in range(2):
            for cond, size in unit_widths(u):
                cols = pl.ds(0, size)

                def early():
                    rs_out[u, d, 2 - d, :, cols] = code4(part_sum[u, d, 1 - d, :, cols])

                when(cond, early)
            rs_send(u, d, pl.ds(2 - d, 1), 4)

    def rs_total(u, size):
        cols = pl.ds(0, size)
        val = part_sum[u, 0, :, :, cols]
        for d in range(2):
            got = rs_in.at[u, d, hop(3), :, cols]
            landed(got, rs_r.at[u, d, 3])
            val = val + decode4(got[...])
        return val.reshape(ROWS, size)

    def tile_cols(t):
        return pl.ds((t % 2) * LANE, LANE)

    def last_gate_up(t):
        if t % 2 == 0:
            wait_hidden(t // 2)

        def go():
            val = rs_total(t, PAIR)
            totals[t] = val
            rows[t // 2, z, :, tile_cols(t)] = first_part(
                val[:, :LANE], val[:, LANE:], hid[t // 2, :, tile_cols(t)]
            )

        when(one(y, t), go)

    def last_tangent(p):
        for cond, size in widths(y, p):

            def go():
                val = rs_total(TILES + p, size)
                for i in range(size // LANE):
                    gate_up, cols = totals[2 * p + i], tile_cols(i)
                    rows[2 + p, z, :, cols] = second_part(
                        gate_up[:, :LANE], gate_up[:, LANE:],
                        val[:, i * LANE : (i + 1) * LANE], hid[p, :, cols],
                    )

            when(cond, go)

    def ag_part(s, d):
        return pl.ds(0, ROWS) if s < 3 else pl.ds(d * HALF, HALF)

    def ag_step(u, s):
        for d in range(2):
            back = s if d == 0 else -s
            blk = mod(z - back, NZ)
            for cond, size in widths(y, u % 2):
                cols = pl.ds(0, size)
                if s > 0:
                    got = rows.at[u, blk, ag_part(s - 1, d), cols]
                    when(cond, lambda: landed(got, ag_r.at[u, d, s - 1]))
                if s < 4:
                    ref = rows.at[u, blk, ag_part(s, d), cols]
                    send(cond, ref, ref, ag_s.at[u], ag_r.at[u, d, s], at_z(z_next[d]))

    outs = (grad_out, curv_out)
    sq[...] = jnp.zeros_like(sq)

    def products(u):
        a, p = u // 2, u % 2
        for i, j in enumerate((2, 1, 3, 0)):
            yy = mod(y + j, NY)
            for cond, size in widths(y, p):
                cols = pl.ds(0, size)

                def go():
                    val = lax.dot_general(
                        tok[:, :, feat(yy)].reshape(NZ * ROWS, FEAT),
                        rows[u, :, :, cols].reshape(NZ * ROWS, size),
                        (((0,), (0,)), ((), ())), preferred_element_type=F32,
                    )
                    if a == 0:
                        squared = jnp.sum((val * val).reshape(FEAT // 8, 8, size), axis=0)
                        for k in range(size // LANE):
                            sq[...] += squared[:, k * LANE : (k + 1) * LANE]
                        outb[u, i, :, cols] = val.astype(BF)
                    else:
                        outb[u, i, :, cols] = code2(val)

                when(cond, go)
                src, dst = outb.at[u, i, :, cols], outs[a].at[:, tile_of(y, 2 * p, size)]
                if j:
                    send(cond, src, dst, gr_s.at[u], gr_r.at[u, j], at_y(yy))
                else:
                    when(cond, pltpu.make_async_copy(src, dst, gr_l.at[u]).start)

    stages = ((sq_z, NZ, z, at_z, 0), (sq_y, NY, y, at_y, 8), (sq_t, 8, tp, at_tp, 12))

    def sum_stage(i):
        if i > 0:
            buf, n, me, _, base = stages[i - 1]
            for r in range(1, n):
                landed(buf.at[mod(me - r, n)], sq_r.at[base + r])
            sq[...] = jnp.sum(buf[...], axis=0)
        if i < len(stages):
            buf, n, me, dev_at, base = stages[i]
            buf[me] = sq[...]
            for r in range(1, n):
                dst = buf.at[me]
                send(None, dst, dst, sq_s.at[i], sq_r.at[base + r], dev_at(mod(me + r, n)))

    pl.when(far_first)(far_tokens)
    wait_weights(0)
    send_hidden(0)
    send_weights(2)
    for step in STEPS:
        kind, i = step[0], int(step[1])
        s = int(step[2:] or 0)
        if kind == "V":
            wait_weights(i)
            if i + 2 < TILES + 2:
                send_weights(i + 2)
            if i == 1:
                send_hidden(1)
        elif kind == "U":
            last_gate_up(i) if s == 4 else rs_step(i, s)
        elif kind == "T":
            last_tangent(i) if s == 4 else rs_step(TILES + i, s)
        elif kind == "G":
            ag_step(i, s)
        elif kind == "H":
            ag_step(2 + i, s)
        elif kind == "P":
            products(i)
        else:
            sum_stage(i)
    squares_out[...] = jnp.broadcast_to(jnp.sum(sq[...]), (8, LANE))

    gone(tok.at[0, :, pl.ds(0, 3 * FEAT)], ty_s)
    gone(tok.at[pl.ds(0, 3)], tx_s)
    gone(tok.at[pl.ds(0, 4)], tc_s)
    for t in range(TILES - 1):
        gone(wu.at[t, :, pl.ds(0, 3 * FEAT), :], wu_s.at[t])
    gone(wt.at[0, pl.ds(0, 3 * FEAT), :], wt_s.at[0])
    for cond, n in ((four_here, 2), (three_here, 4)):
        when(cond, lambda: gone(wu.at[TILES - 1, :, pl.ds(0, n * FEAT // 2), :], wu_s.at[TILES - 1]))
        when(cond, lambda: gone(wt.at[1, pl.ds(0, FEAT * (n + 6) // 4), :], wt_s.at[1]))
    for r in range(1, NY):
        yy = mod(y + r, NY)
        for p in range(2):
            for cond, size in widths(yy, p):
                when(cond, lambda: gone(hid.at[p, my_toks, pl.ds(0, size)], hid_s.at[p, r]))
    for i, (buf, n, _, _, _) in enumerate(stages):
        gone(buf.at[pl.ds(0, n - 1)], sq_s.at[i])
    for u in range(6):
        for cond, size in unit_widths(u):
            when(cond, lambda: gone(rs_out.at[u, :, :, :, pl.ds(0, size)], rs_s.at[u]))
    for u in range(4):
        for cond, size in widths(y, u % 2):
            when(cond, lambda: gone(rows.at[u, pl.ds(0, 7), :, pl.ds(0, size)], ag_s.at[u]))
    for u in ENDS:
        a, p = u // 2, u % 2
        for cond, size in widths(y, p):
            cols = pl.ds(0, size)

            def go():
                src, dst = outb.at[u, 3, :, cols], outs[a].at[:, tile_of(y, 2 * p, size)]
                pltpu.make_async_copy(src, dst, gr_l.at[u]).wait()
                gone(outb.at[u, pl.ds(0, 3), :, cols], gr_s.at[u])

            when(cond, go)
        for j in range(1, NY):
            yy = mod(y - j, NY)
            for cond, size in widths(yy, p):
                got = outs[a].at[:, tile_of(yy, 2 * p, size)]
                when(cond, lambda: landed(got, gr_r.at[u, j]))


def products_of(tokens, hidden_grad, gate_weight, up_weight, probe):
    dma = pltpu.SemaphoreType.DMA
    hbm = pl.BlockSpec(memory_space=pl.ANY)
    far = pl.BlockSpec(memory_space=pltpu.HBM)
    return pl.pallas_call(
        kernel,
        out_shape=(
            jax.ShapeDtypeStruct((FEAT, 14 * LANE), BF),
            jax.ShapeDtypeStruct((FEAT, 14 * LANE), BF),
            jax.ShapeDtypeStruct((8, LANE), F32),
        ),
        in_specs=[far] * 5,
        out_specs=(hbm, hbm, pl.BlockSpec(memory_space=pltpu.VMEM)),
        scratch_shapes=[
            pltpu.VMEM((8, ROWS, DEPTH), BF),
            pltpu.VMEM((3, FEAT, 14 * LANE), BF),
            pltpu.VMEM((TILES, 2, DEPTH, LANE), BF),
            pltpu.VMEM((2, DEPTH, PAIR), BF),
            pltpu.VMEM((2, ROWS, PAIR), BF),
            pltpu.VMEM((6, 2, 2, HALF, PAIR), F32),
            pltpu.VMEM((TILES, ROWS, PAIR), F32),
            pltpu.VMEM((6, 2, 7, HALF, PAIR), BF),
            pltpu.VMEM((6, 2, 7, HALF, PAIR), BF),
            pltpu.VMEM((4, NZ, ROWS, PAIR), BF),
            pltpu.VMEM((4, NY, FEAT, PAIR), BF),
            pltpu.VMEM((8, LANE), F32),
            pltpu.VMEM((NZ, 8, LANE), F32),
            pltpu.VMEM((NY, 8, LANE), F32),
            pltpu.VMEM((8, 8, LANE), F32),
            dma, dma, dma((NY,)), dma, dma((3, NY)), dma, dma((8,)), dma((3,)),
            dma((TILES,)), dma((TILES,)), dma((TILES, NY)), dma((2,)), dma((2,)), dma((2, NY)),
            dma((2,)), dma((2, NY)), dma((2, NY)),
            dma((6,)), dma((6, 2, 5)), dma((4,)), dma((4, 2, 4)),
            dma((4,)), dma((4,)), dma((4, NY)), dma((3,)), dma((20,)),
        ],
        compiler_params=pltpu.CompilerParams(
            collective_id=0, has_side_effects=True, vmem_limit_bytes=62 * 1024 * 1024
        ),
    )(tokens, hidden_grad, gate_weight, up_weight, probe)


def finish(squares, grad, curv, probe, moment, curvature, moment_out, curvature_out, update_out):
    factor = jnp.minimum(1.0, lax.rsqrt(squares[0:1, 0:1] / (D * FF) + mean_eps))
    new_moment = moment_decay * moment[...] + (1.0 - moment_decay) * factor * grad[...].astype(F32)
    new_curvature = curvature_decay * curvature[...] + (
        1.0 - curvature_decay
    ) * factor * probe[...].astype(F32) * decode2(curv[...])
    moment_out[...] = new_moment
    curvature_out[...] = new_curvature
    update_out[...] = jnp.clip(
        new_moment / jnp.maximum(curvature_scale * new_curvature, ratio_floor), -1.0, 1.0
    )


def body(tokens, hidden_grad, gate_weight, up_weight, probe, moment, curvature):
    gradient, curv_coded, squares = products_of(tokens, hidden_grad, gate_weight, up_weight, probe)
    part = pl.BlockSpec((128, 14 * LANE), lambda i: (i, 0))
    return pl.pallas_call(
        finish,
        grid=(FEAT // 128,),
        out_shape=[jax.ShapeDtypeStruct((FEAT, 14 * LANE), F32)] * 3,
        in_specs=[pl.BlockSpec((8, LANE), lambda i: (0, 0))] + [part] * 5,
        out_specs=[part] * 3,
        compiler_params=pltpu.CompilerParams(vmem_limit_bytes=62 * 1024 * 1024),
    )(squares, gradient, curv_coded, probe, moment, curvature)


def solution(mesh):
    placed = (
        P("tp", "dp"),
        P("dp", "tp"),
        P("dp", "tp"),
        P("dp", "tp"),
        P("dp", "tp"),
        P("dp", "tp"),
        P("dp", "tp"),
    )
    return jax.shard_map(
        body,
        mesh=mesh,
        in_specs=placed,
        out_specs=(P("dp", "tp"), P("dp", "tp"), P("dp", "tp")),
        check_vma=False,
    )
```

```python
import functools

import jax
import jax.numpy as jnp
from jax import lax
from jax.experimental import pallas as pl
from jax.experimental.pallas import tpu as pltpu
from jax.sharding import PartitionSpec as P

D = 8192
FF = 14336

moment_decay = 0.9
curvature_decay = 0.99
curvature_scale = 2.0
ratio_floor = 0.05
mean_eps = 1e-06

NX, NY, NZ = 4, 4, 8
ROWS = 192
HALF = 96
FEAT = 256
DEPTH = NY * FEAT
LANE = 128
PAIR = 2 * LANE
TILES = 4

BF = jnp.bfloat16
F32 = jnp.float32


def first_part(gate_pre, up_value, upstream):
    sigmoid_val = jax.nn.sigmoid(gate_pre)
    first_deriv = sigmoid_val * (1.0 + gate_pre * (1.0 - sigmoid_val))
    return (upstream.astype(F32) * up_value * first_deriv).astype(BF)


def second_part(gate_pre, up_value, tangent, upstream):
    sigmoid_val = jax.nn.sigmoid(gate_pre)
    second_deriv = sigmoid_val * (1.0 - sigmoid_val) * (2.0 + gate_pre * (1.0 - 2.0 * sigmoid_val))
    return (upstream.astype(F32) * up_value * second_deriv * tangent).astype(BF)


def code4(val):
    return ((val * jnp.abs(val)) * (val * val)).astype(BF)


def decode4(coded):
    val = coded.astype(F32)
    root = lax.rsqrt(jnp.maximum(jnp.abs(val), 1e-36))
    return val * root * root * lax.rsqrt(root)


def code2(val):
    return (val * jnp.abs(val)).astype(BF)


def decode2(coded):
    val = coded.astype(F32)
    return val * lax.rsqrt(jnp.maximum(jnp.abs(val), 1e-36))


STEPS = (
    "U00", "V1", "U10", "U01", "U11", "V2", "U20", "U02", "V3", "U30", "U12", "U21", "U31", "U03", "U13",
    "V4", "V5", "T10", "U22", "T00", "U32", "T11", "U04", "U14", "G00", "T01", "U23", "U33", "T12", "G01",
    "T02", "U24", "U34", "G10", "T13", "G02", "T03", "G11", "T14", "H10", "G03", "T04", "G12", "H11", "G04",
    "H00", "P0", "G13", "H12", "G14", "H01", "P1", "S0", "H13", "H02", "H14", "P3", "H03", "S1", "H04",
    "P2", "S2", "S3",
)
ENDS = tuple(int(step[1]) for step in STEPS if step[0] == "P")


def kernel(
    tok_in, hid_in, gate_in, up_in, probe_in,
    grad_out, curv_out, squares_out,
    tok, wsrc, wu, wt, hid, part_sum, totals, rs_out, rs_in, rows, outb, sq, sq_z, sq_y, sq_t,
    tok_l, ty_s, ty_r, tx_s, tx_r, tc_s, tc_r, src_l, wu_l, wu_s, wu_r, wt_l, wt_s, wt_r,
    hid_l, hid_s, hid_r, rs_s, rs_r, ag_s, ag_r, gr_l, gr_s, gr_r, sq_s, sq_r,
):
    tp, dp = lax.axis_index("tp"), lax.axis_index("dp")
    x, c = lax.div(tp, 2), lax.rem(tp, 2)
    z, y = lax.div(dp, NY), lax.rem(dp, NY)

    def mod(val, n):
        return lax.rem(val + n, n)

    def at_y(yy):
        return {"dp": z * NY + yy}

    def at_z(zz):
        return {"dp": zz * NY + y}

    def at_tp(tt):
        return {"tp": tt}

    def first_tile(yy):
        return lax.div(7 * yy + 1 - c, 2)

    def four(yy):
        return lax.rem(yy + c, 2) == 0

    four_here, three_here = four(y), lax.rem(y + c, 2) == 1

    def one(yy, t):
        return four(yy) if t == TILES - 1 else None

    def widths(yy, p):
        if p == 0:
            return ((None, PAIR),)
        return ((four(yy), PAIR), (lax.rem(yy + c, 2) == 1, LANE))

    def when(cond, fn):
        if cond is None:
            fn()
        else:
            pl.when(cond)(fn)

    def lanes(start, size):
        return pl.ds(pl.multiple_of(start, LANE), size)

    def tile_of(yy, t, size=LANE):
        return lanes((first_tile(yy) + t) * LANE, size)

    def feat(yy):
        return lanes(yy * FEAT, FEAT)

    def remote(src, dst, s_sem, r_sem, dev):
        return pltpu.make_async_remote_copy(
            src_ref=src, dst_ref=dst, send_sem=s_sem, recv_sem=r_sem,
            device_id=dev, device_id_type=pl.DeviceIdType.MESH,
        )

    def send(cond, *args):
        when(cond, remote(*args).start)

    def landed(dst, r_sem):
        remote(dst, dst, r_sem, r_sem, at_tp(tp)).wait_recv()

    def gone(src, s_sem):
        remote(src, src, s_sem, s_sem, at_tp(tp)).wait_send()

    tok_own = pltpu.make_async_copy(tok_in, tok.at[tp, :, feat(y)], tok_l)
    tok_own.start()
    weights = (gate_in, up_in, probe_in)
    staged = [pltpu.make_async_copy(weights[a], wsrc.at[a], src_l.at[a]) for a in range(3)]
    for copy in staged:
        copy.start()
    my_toks = pl.ds(pl.multiple_of(y * 48, 48), 48)

    def hid_own(p, size):
        return pltpu.make_async_copy(
            hid_in.at[:, tile_of(y, 2 * p, size)],
            hid.at[p, my_toks, pl.ds(0, size)],
            hid_l.at[p],
        )

    for p in range(2):
        for cond, size in widths(y, p):
            when(cond, hid_own(p, size).start)

    barrier = pltpu.get_barrier_semaphore()
    peers = [at_y(mod(y + r, NY)) for r in range(1, NY)]
    peers += [at_z(mod(z + r, NZ)) for r in range(1, NZ)]
    peers += [at_tp(mod(tp + r, 8)) for r in range(1, 8)]
    for dev in peers:
        pl.semaphore_signal(barrier, inc=1, device_id=dev, device_id_type=pl.DeviceIdType.MESH)
    pl.semaphore_wait(barrier, len(peers))

    x_next = (mod(tp + 2, 8), mod(tp - 2, 8))
    far = mod(tp + 4, 8)
    other = tp + 1 - 2 * c

    def x_send(blk, r, d, slot):
        ref = tok.at[blk, :, feat(mod(y - r, NY))]
        send(None, ref, ref, tx_s, tx_r.at[slot, r], at_tp(x_next[d]))

    def x_landed(blk, r, slot):
        landed(tok.at[blk, :, feat(mod(y - r, NY))], tx_r.at[slot, r])

    def core_send(blk):
        send(None, tok.at[blk], tok.at[blk], tc_s, tc_r.at[blk], at_tp(other))

    for r in (1, 3, 2):
        send(None, tok_in, tok.at[tp, :, feat(y)], ty_s, ty_r.at[r], at_y(mod(y + r, NY)))
    tok_own.wait()
    for d in range(2):
        x_send(tp, 0, d, d)
    for copy in staged:
        copy.wait()

    def wu_own(t):
        src, dst = wsrc.at[pl.ds(0, 2), :, tile_of(y, t)], wu.at[t, :, feat(y), :]
        return pltpu.make_async_copy(src, dst, wu_l.at[t])

    def wt_own(p, size):
        src, dst = wsrc.at[2, :, tile_of(y, 2 * p, size)], wt.at[p, feat(y), pl.ds(0, size)]
        return pltpu.make_async_copy(src, dst, wt_l.at[p])

    def send_weights(i):
        for r in (2, 1, 3):
            yy = mod(y + r, NY)
            if i < TILES:
                src, dst = wsrc.at[pl.ds(0, 2), :, tile_of(yy, i)], wu.at[i, :, feat(y), :]
                send(one(yy, i), src, dst, wu_s.at[i], wu_r.at[i, r], at_y(yy))
            else:
                p = i - TILES
                for cond, size in widths(yy, p):
                    src = wsrc.at[2, :, tile_of(yy, 2 * p, size)]
                    dst = wt.at[p, feat(y), pl.ds(0, size)]
                    send(cond, src, dst, wt_s.at[p], wt_r.at[p, r], at_y(yy))
        if i < TILES:
            when(one(y, i), wu_own(i).start)
        else:
            for cond, size in widths(y, i - TILES):
                when(cond, wt_own(i - TILES, size).start)

    def wait_weights(i):
        if i < TILES:

            def go():
                wu_own(i).wait()
                for r in range(1, NY):
                    landed(wu.at[i, :, feat(mod(y - r, NY)), :], wu_r.at[i, r])

            when(one(y, i), go)
            return
        p = i - TILES
        for cond, size in widths(y, p):

            def go():
                wt_own(p, size).wait()
                for r in range(1, NY):
                    landed(wt.at[p, feat(mod(y - r, NY)), pl.ds(0, size)], wt_r.at[p, r])

            when(cond, go)

    def send_hidden(p):
        for r in range(1, NY):
            yy = mod(y + r, NY)
            for cond, size in widths(yy, p):
                src = hid_in.at[:, tile_of(yy, 2 * p, size)]
                dst = hid.at[p, my_toks, pl.ds(0, size)]
                send(cond, src, dst, hid_s.at[p, r], hid_r.at[p, r], at_y(yy))

    def wait_hidden(p):
        for cond, size in widths(y, p):

            def go():
                hid_own(p, size).wait()
                for r in range(1, NY):
                    toks = pl.ds(pl.multiple_of(mod(y - r, NY) * 48, 48), 48)
                    landed(hid.at[p, toks, pl.ds(0, size)], hid_r.at[p, r])

            when(cond, go)

    for r in (1, 3, 2):
        landed(tok.at[tp, :, feat(mod(y - r, NY))], ty_r.at[r])
        for d in range(2):
            x_send(tp, r, d, d)
        if r == 3:
            send_weights(0)
    core_send(tp)
    for d, r in ((0, 0), (0, 1), (1, 3), (1, 2)):
        x_landed(x_next[1 - d], r, d)
        x_send(x_next[1 - d], r, d, 2)
    send_weights(1)
    for d, rest in ((0, (3, 2)), (1, (0, 1))):
        for r in rest:
            x_landed(x_next[1 - d], r, d)
        core_send(x_next[1 - d])

    def far_tokens():
        for r in (0, 1, 3, 2):
            x_landed(far, r, 2)
        core_send(far)

    far_first = lax.div(mod(z + 4, NZ), 2) == lax.div(far, 2)
    far_later = lax.div(mod(z + 4, NZ), 2) != lax.div(far, 2)

    def wait_block(blk):
        pl.when(lax.rem(blk, 2) != c)(lambda: landed(tok.at[blk], tc_r.at[blk]))

    z_next = (mod(z + 1, NZ), mod(z - 1, NZ))

    def unit_widths(u):
        if u >= TILES:
            return widths(y, u - TILES)
        return ((one(y, u), PAIR),)

    def hop(s):
        return pl.ds(0, 1) if s == 0 else pl.ds(2 * s - 1, 2)

    def dots(u, s):
        if s in (0, 4):
            blks = (mod(z + 4 - s, NZ),)
        else:
            blks = (mod(z + 4 - s, NZ), mod(z - 4 + s, NZ))
        for d, blk in enumerate(blks):
            if u == 0:
                wait_block(blk)
            for cond, size in unit_widths(u):

                def go():
                    if u < TILES:
                        wide = jnp.concatenate([wu[u, a] for a in range(2)], axis=1)
                    else:
                        wide = wt[u - TILES, :, pl.ds(0, size)]
                    val = jnp.dot(tok[blk], wide, preferred_element_type=F32)
                    part_sum[u, d, :, :, pl.ds(0, size)] = val.reshape(2, HALF, size)

                when(cond, go)

    def rs_send(u, d, at, sem):
        for cond, size in unit_widths(u):
            cols = pl.ds(0, size)
            src, dst = rs_out.at[u, d, at, :, cols], rs_in.at[u, d, at, :, cols]
            send(cond, src, dst, rs_s.at[u], rs_r.at[u, d, sem], at_z(z_next[d]))

    def rs_step(u, s):
        if s == 0:
            dots(u, 0)
        for d in range(2):
            at = pl.ds(1 + d, 1) if s == 1 else hop(s)
            for cond, size in unit_widths(u):
                cols = pl.ds(0, size)

                def go():
                    if s == 0:
                        rs_out[u, d, 0, :, cols] = code4(part_sum[u, 0, d, :, cols])
                        return
                    part = pl.ds(d, 1) if s == 1 else pl.ds(0, 2)
                    if s == 2:
                        landed(rs_in.at[u, d, pl.ds(1 + d, 1), :, cols], rs_r.at[u, d, 1])
                        landed(rs_in.at[u, d, pl.ds(2 - d, 1), :, cols], rs_r.at[u, d, 4])
                    else:
                        landed(rs_in.at[u, d, hop(s - 1), :, cols], rs_r.at[u, d, s - 1])
                    val = part_sum[u, d, part, :, cols] + decode4(rs_in[u, d, hop(s - 1), :, cols])
                    rs_out[u, d, at, :, cols] = code4(val)

                when(cond, go)
            rs_send(u, d, at, s)
        if u == 0 and s == 0:
            pl.when(far_later)(far_tokens)
        dots(u, s + 1)
        if s > 0:
            return
        for d in range(2):
            for cond, size in unit_widths(u):
                cols = pl.ds(0, size)

                def early():
                    rs_out[u, d, 2 - d, :, cols] = code4(part_sum[u, d, 1 - d, :, cols])

                when(cond, early)
            rs_send(u, d, pl.ds(2 - d, 1), 4)

    def rs_total(u, size):
        cols = pl.ds(0, size)
        val = part_sum[u, 0, :, :, cols]
        for d in range(2):
            got = rs_in.at[u, d, hop(3), :, cols]
            landed(got, rs_r.at[u, d, 3])
            val = val + decode4(got[...])
        return val.reshape(ROWS, size)

    def tile_cols(t):
        return pl.ds((t % 2) * LANE, LANE)

    def last_gate_up(t):
        if t % 2 == 0:
            wait_hidden(t // 2)

        def go():
            val = rs_total(t, PAIR)
            totals[t] = val
            rows[t // 2, z, :, tile_cols(t)] = first_part(
                val[:, :LANE], val[:, LANE:], hid[t // 2, :, tile_cols(t)]
            )

        when(one(y, t), go)

    def last_tangent(p):
        for cond, size in widths(y, p):

            def go():
                val = rs_total(TILES + p, size)
                for i in range(size // LANE):
                    gate_up, cols = totals[2 * p + i], tile_cols(i)
                    rows[2 + p, z, :, cols] = second_part(
                        gate_up[:, :LANE], gate_up[:, LANE:],
                        val[:, i * LANE : (i + 1) * LANE], hid[p, :, cols],
                    )

            when(cond, go)

    def ag_part(s, d):
        return pl.ds(0, ROWS) if s < 3 else pl.ds(d * HALF, HALF)

    def ag_step(u, s):
        for d in range(2):
            back = s if d == 0 else -s
            blk = mod(z - back, NZ)
            for cond, size in widths(y, u % 2):
                cols = pl.ds(0, size)
                if s > 0:
                    got = rows.at[u, blk, ag_part(s - 1, d), cols]
                    when(cond, lambda: landed(got, ag_r.at[u, d, s - 1]))
                if s < 4:
                    ref = rows.at[u, blk, ag_part(s, d), cols]
                    send(cond, ref, ref, ag_s.at[u], ag_r.at[u, d, s], at_z(z_next[d]))

    outs = (grad_out, curv_out)
    sq[...] = jnp.zeros_like(sq)

    def products(u):
        a, p = u // 2, u % 2
        for i, j in enumerate((2, 1, 3, 0)):
            yy = mod(y + j, NY)
            for cond, size in widths(y, p):
                cols = pl.ds(0, size)

                def go():
                    val = lax.dot_general(
                        tok[:, :, feat(yy)].reshape(NZ * ROWS, FEAT),
                        rows[u, :, :, cols].reshape(NZ * ROWS, size),
                        (((0,), (0,)), ((), ())), preferred_element_type=F32,
                    )
                    if a == 0:
                        squared = jnp.sum((val * val).reshape(FEAT // 8, 8, size), axis=0)
                        for k in range(size // LANE):
                            sq[...] += squared[:, k * LANE : (k + 1) * LANE]
                        outb[u, i, :, cols] = val.astype(BF)
                    else:
                        outb[u, i, :, cols] = code2(val)

                when(cond, go)
                src, dst = outb.at[u, i, :, cols], outs[a].at[:, tile_of(y, 2 * p, size)]
                if j:
                    send(cond, src, dst, gr_s.at[u], gr_r.at[u, j], at_y(yy))
                else:
                    when(cond, pltpu.make_async_copy(src, dst, gr_l.at[u]).start)

    stages = ((sq_z, NZ, z, at_z, 0), (sq_y, NY, y, at_y, 8), (sq_t, 8, tp, at_tp, 12))

    def sum_stage(i):
        if i > 0:
            buf, n, me, _, base = stages[i - 1]
            for r in range(1, n):
                landed(buf.at[mod(me - r, n)], sq_r.at[base + r])
            sq[...] = jnp.sum(buf[...], axis=0)
        if i < len(stages):
            buf, n, me, dev_at, base = stages[i]
            buf[me] = sq[...]
            for r in range(1, n):
                dst = buf.at[me]
                send(None, dst, dst, sq_s.at[i], sq_r.at[base + r], dev_at(mod(me + r, n)))

    pl.when(far_first)(far_tokens)
    wait_weights(0)
    send_hidden(0)
    send_weights(2)
    for step in STEPS:
        kind, i = step[0], int(step[1])
        s = int(step[2:] or 0)
        if kind == "V":
            wait_weights(i)
            if i + 2 < TILES + 2:
                send_weights(i + 2)
            if i == 1:
                send_hidden(1)
        elif kind == "U":
            last_gate_up(i) if s == 4 else rs_step(i, s)
        elif kind == "T":
            last_tangent(i) if s == 4 else rs_step(TILES + i, s)
        elif kind == "G":
            ag_step(i, s)
        elif kind == "H":
            ag_step(2 + i, s)
        elif kind == "P":
            products(i)
        else:
            sum_stage(i)
    squares_out[...] = jnp.broadcast_to(jnp.sum(sq[...]), (8, LANE))

    gone(tok.at[0, :, pl.ds(0, 3 * FEAT)], ty_s)
    gone(tok.at[pl.ds(0, 3)], tx_s)
    gone(tok.at[pl.ds(0, 4)], tc_s)
    for t in range(TILES - 1):
        gone(wu.at[t, :, pl.ds(0, 3 * FEAT), :], wu_s.at[t])
    gone(wt.at[0, pl.ds(0, 3 * FEAT), :], wt_s.at[0])
    for cond, n in ((four_here, 2), (three_here, 4)):
        when(cond, lambda: gone(wu.at[TILES - 1, :, pl.ds(0, n * FEAT // 2), :], wu_s.at[TILES - 1]))
        when(cond, lambda: gone(wt.at[1, pl.ds(0, FEAT * (n + 6) // 4), :], wt_s.at[1]))
    for r in range(1, NY):
        yy = mod(y + r, NY)
        for p in range(2):
            for cond, size in widths(yy, p):
                when(cond, lambda: gone(hid.at[p, my_toks, pl.ds(0, size)], hid_s.at[p, r]))
    for i, (buf, n, _, _, _) in enumerate(stages):
        gone(buf.at[pl.ds(0, n - 1)], sq_s.at[i])
    for u in range(6):
        for cond, size in unit_widths(u):
            when(cond, lambda: gone(rs_out.at[u, :, :, :, pl.ds(0, size)], rs_s.at[u]))
    for u in range(4):
        for cond, size in widths(y, u % 2):
            when(cond, lambda: gone(rows.at[u, pl.ds(0, 7), :, pl.ds(0, size)], ag_s.at[u]))
    for u in ENDS:
        a, p = u // 2, u % 2
        for cond, size in widths(y, p):
            cols = pl.ds(0, size)

            def go():
                src, dst = outb.at[u, 3, :, cols], outs[a].at[:, tile_of(y, 2 * p, size)]
                pltpu.make_async_copy(src, dst, gr_l.at[u]).wait()
                gone(outb.at[u, pl.ds(0, 3), :, cols], gr_s.at[u])

            when(cond, go)
        for j in range(1, NY):
            yy = mod(y - j, NY)
            for cond, size in widths(yy, p):
                got = outs[a].at[:, tile_of(yy, 2 * p, size)]
                when(cond, lambda: landed(got, gr_r.at[u, j]))


def products_of(tokens, hidden_grad, gate_weight, up_weight, probe):
    dma = pltpu.SemaphoreType.DMA
    hbm = pl.BlockSpec(memory_space=pl.ANY)
    far = pl.BlockSpec(memory_space=pltpu.HBM)
    return pl.pallas_call(
        kernel,
        out_shape=(
            jax.ShapeDtypeStruct((FEAT, 14 * LANE), BF),
            jax.ShapeDtypeStruct((FEAT, 14 * LANE), BF),
            jax.ShapeDtypeStruct((8, LANE), F32),
        ),
        in_specs=[far] * 5,
        out_specs=(hbm, hbm, pl.BlockSpec(memory_space=pltpu.VMEM)),
        scratch_shapes=[
            pltpu.VMEM((8, ROWS, DEPTH), BF),
            pltpu.VMEM((3, FEAT, 14 * LANE), BF),
            pltpu.VMEM((TILES, 2, DEPTH, LANE), BF),
            pltpu.VMEM((2, DEPTH, PAIR), BF),
            pltpu.VMEM((2, ROWS, PAIR), BF),
            pltpu.VMEM((6, 2, 2, HALF, PAIR), F32),
            pltpu.VMEM((TILES, ROWS, PAIR), F32),
            pltpu.VMEM((6, 2, 7, HALF, PAIR), BF),
            pltpu.VMEM((6, 2, 7, HALF, PAIR), BF),
            pltpu.VMEM((4, NZ, ROWS, PAIR), BF),
            pltpu.VMEM((4, NY, FEAT, PAIR), BF),
            pltpu.VMEM((8, LANE), F32),
            pltpu.VMEM((NZ, 8, LANE), F32),
            pltpu.VMEM((NY, 8, LANE), F32),
            pltpu.VMEM((8, 8, LANE), F32),
            dma, dma, dma((NY,)), dma, dma((3, NY)), dma, dma((8,)), dma((3,)),
            dma((TILES,)), dma((TILES,)), dma((TILES, NY)), dma((2,)), dma((2,)), dma((2, NY)),
            dma((2,)), dma((2, NY)), dma((2, NY)),
            dma((6,)), dma((6, 2, 5)), dma((4,)), dma((4, 2, 4)),
            dma((4,)), dma((4,)), dma((4, NY)), dma((3,)), dma((20,)),
        ],
        compiler_params=pltpu.CompilerParams(
            collective_id=0, has_side_effects=True, vmem_limit_bytes=62 * 1024 * 1024
        ),
    )(tokens, hidden_grad, gate_weight, up_weight, probe)


def finish(squares, grad, curv, probe, moment, curvature, moment_out, curvature_out, update_out):
    factor = jnp.minimum(1.0, lax.rsqrt(squares[0:1, 0:1] / (D * FF) + mean_eps))
    new_moment = moment_decay * moment[...] + (1.0 - moment_decay) * factor * grad[...].astype(F32)
    new_curvature = curvature_decay * curvature[...] + (
        1.0 - curvature_decay
    ) * factor * probe[...].astype(F32) * decode2(curv[...])
    moment_out[...] = new_moment
    curvature_out[...] = new_curvature
    update_out[...] = jnp.clip(
        new_moment / jnp.maximum(curvature_scale * new_curvature, ratio_floor), -1.0, 1.0
    )


def body(tokens, hidden_grad, gate_weight, up_weight, probe, moment, curvature):
    gradient, curv_coded, squares = products_of(tokens, hidden_grad, gate_weight, up_weight, probe)
    part = pl.BlockSpec((128, 14 * LANE), lambda i: (i, 0))
    return pl.pallas_call(
        finish,
        grid=(FEAT // 128,),
        out_shape=[jax.ShapeDtypeStruct((FEAT, 14 * LANE), F32)] * 3,
        in_specs=[pl.BlockSpec((8, LANE), lambda i: (0, 0))] + [part] * 5,
        out_specs=[part] * 3,
        compiler_params=pltpu.CompilerParams(vmem_limit_bytes=62 * 1024 * 1024),
    )(squares, gradient, curv_coded, probe, moment, curvature)


def solution(mesh):
    placed = (
        P("tp", "dp"),
        P("dp", "tp"),
        P("dp", "tp"),
        P("dp", "tp"),
        P("dp", "tp"),
        P("dp", "tp"),
        P("dp", "tp"),
    )
    return jax.shard_map(
        body,
        mesh=mesh,
        in_specs=placed,
        out_specs=(P("dp", "tp"), P("dp", "tp"), P("dp", "tp")),
        check_vma=False,
    )
```
